32 devices in a mesh: gene: 8 (over z, y), cell: 4 (over x, core).
Axes of the slice: x: 2, y: 2, z: 4, core: 2. Of those that a mesh axis runs over, the one named last changes fastest.
Arguments:
- counts: bfloat16 [4096, 1792], P('cell', 'gene'), may hold values from -12 to 12
- study: int32 [4096], P('cell'), may hold values from 0 to 7
- study_gene_mask: int32 [8, 1792], P(None, 'gene'), may hold values 0 or 1
- noise: float32 [4096, 100], P(('cell', 'gene')), may hold values from -5 to 5
- enc_in: float32 [1792, 800], P('gene'), may hold values from -0.125 to 0.125
- enc_mid: float32 [800, 800], replicated, may hold values from -0.21875 to 0.21875
- latent_w: float32 [2, 800, 100], replicated, may hold values from -0.21875 to 0.21875
- dec_in: float32 [100, 800], replicated, may hold values from -0.625 to 0.625
- dec_mid: float32 [800, 800], replicated, may hold values from -0.21875 to 0.21875
- dec_out: float32 [800, 1792], P(None, 'gene'), may hold values from -0.21875 to 0.21875
- norm_params: float32 [2, 4, 800], replicated, may hold values from 0.5 to 1.5
- latent_bias: float32 [2, 100], replicated, may hold values from -3 to 3
- out_bias: float32 [1792], P('gene'), may hold values from -3 to 3
- running_mean: float32 [4, 800], replicated, may hold values from -3 to 3
- running_variance: float32 [4, 800], replicated, may hold values from 0.5 to 4
- mom_enc_in: float32 [1792, 800], P('gene'), may hold values from -1.5 to 1.5
- mom_enc_mid: float32 [800, 800], replicated, may hold values from -0.75 to 0.75
- mom_latent_w: float32 [2, 800, 100], replicated, may hold values from -2 to 2
- mom_dec_in: float32 [100, 800], replicated, may hold values from -0.75 to 0.75
- mom_dec_mid: float32 [800, 800], replicated, may hold values from -0.75 to 0.75
- mom_dec_out: float32 [800, 1792], P(None, 'gene'), may hold values from -0.5 to 0.5
- mom_norm: float32 [2, 4, 800], replicated, may hold values from -0.75 to 0.75
- mom_latent_bias: float32 [2, 100], replicated, may hold values from -2 to 2
- mom_out_bias: float32 [1792], P('gene'), may hold values from -1 to 1
Outputs:
- recon: bfloat16 [4096, 1792], P('cell', 'gene')
- loss: float32 [], replicated
- new_enc_in: float32 [1792, 800], P('gene')
- new_mom_enc_in: float32 [1792, 800], P('gene')
- new_enc_mid: float32 [800, 800], replicated
- new_mom_enc_mid: float32 [800, 800], replicated
- new_latent_w: float32 [2, 800, 100], replicated
- new_mom_latent_w: float32 [2, 800, 100], replicated
- new_dec_in: float32 [100, 800], replicated
- new_mom_dec_in: float32 [100, 800], replicated
- new_dec_mid: float32 [800, 800], replicated
- new_mom_dec_mid: float32 [800, 800], replicated
- new_dec_out: float32 [800, 1792], P(None, 'gene')
- new_mom_dec_out: float32 [800, 1792], P(None, 'gene')
- new_norm_params: float32 [2, 4, 800], replicated
- new_mom_norm: float32 [2, 4, 800], replicated
- new_latent_bias: float32 [2, 100], replicated
- new_mom_latent_bias: float32 [2, 100], replicated
- new_out_bias: float32 [1792], P('gene')
- new_mom_out_bias: float32 [1792], P('gene')
- new_running_mean: float32 [4, 800], replicated
- updated_running_variance: float32 [4, 800], replicated
The draws below stay inside these ranges and needn't reach their ends.
All inputs are finite; a program needn't handle non-finite values. No bound on the sum of `study_gene_mask` on one device may be relied on, other than what follows from the above.
Results may differ from the reference program's by a relative error of at most 0.013.
Values may be sent and summed in bfloat16 or wider, within the bound.
No kernel may reach another device: no remote copies, remote signals or barrier semaphores. Data moves between devices by JAX's collectives and lax.ppermute only.
A program may use at most 192 MiB of HBM per device.

```python
import math
import jax
import jax.numpy as jnp
from jax import lax

G = 1792
H = 800
Z = 100
S = 8
NS = 5
CELLS = 4096


def draw_counts(key, part):
    key = jax.random.fold_in(key, 11)
    sample_base = jnp.clip(jax.random.normal(key, (CELLS, G), jnp.float32), -4.0, 4.0)
    growth = 3.0
    row_scale = growth ** (0.5 * jnp.arange(CELLS, dtype=jnp.float32) / (CELLS - 1))
    gene_scale = growth ** (0.5 * jnp.arange(G, dtype=jnp.float32) / (G - 1))
    return (sample_base * row_scale[:, None] * gene_scale[None, :]).astype(jnp.bfloat16)


def touch_ends(entries, own_key, least, largest):
    longest = entries.shape.index(max(entries.shape))
    spots = []
    for shift in (0, 1):
        where = [jax.random.randint(jax.random.fold_in(own_key, axis), (), 0, length) for axis, length in enumerate(entries.shape)]
        where[longest] = (where[longest] + shift) % entries.shape[longest]
        spots.append(tuple(where))
    return entries.at[spots[0]].set(least).at[spots[1]].set(largest)


def shard_levels(stream_key, shape, cuts, low, top_value):
    factor_of = 1.0
    for axis_at, blocks in cuts:
        steps = jax.random.uniform(jax.random.fold_in(jax.random.fold_in(stream_key, 6), axis_at), (blocks,), jnp.float32, low / len(cuts), top_value / len(cuts))
        factor_of = factor_of * jnp.repeat(jnp.exp(steps), shape[axis_at] // blocks).reshape((-1,) + (1,) * (len(shape) - 1 - axis_at))
    return factor_of


def normal_values(key, shape, spread, bound, pieces=(), kind=jnp.bfloat16):
    values = jax.random.normal(key, shape, jnp.float32) * spread
    if len(pieces) > 0:
        values = shard_levels(key, shape, pieces, -0.22, 0.18) * values
    return jnp.clip(values, min=-bound, max=bound).astype(kind)


def setup_inputs(seed: int = 0) -> dict:
    splits = jax.random.split(jax.random.key(seed), 25)
    counts = draw_counts(jax.random.fold_in(splits[24], 71), 0)
    study = touch_ends(jax.random.randint(splits[1], (CELLS,), 0, S), jax.random.fold_in(splits[1], 1), 0, S - 1).astype(jnp.int32)
    study_gene_mask = touch_ends((jax.random.randint(splits[2], (S, G), 0, 4) < 3).astype(jnp.int32), jax.random.fold_in(splits[2], 1), 0, 1)
    noise = normal_values(splits[3], (CELLS, Z), 1.0, 5.0, ((0, 32),), jnp.float32)
    enc_in = normal_values(splits[4], (G, H), G ** -0.5, 0.125, ((0, 8),), jnp.float32)
    enc_mid = normal_values(splits[5], (H, H), H ** -0.5, 0.21875, (), jnp.float32)
    latent_w = normal_values(splits[6], (2, H, Z), H ** -0.5, 0.21875, (), jnp.float32)
    dec_in = normal_values(splits[7], (Z, H), Z ** -0.5, 0.625, (), jnp.float32)
    dec_mid = normal_values(splits[8], (H, H), H ** -0.5, 0.21875, (), jnp.float32)
    dec_out = normal_values(splits[9], (H, G), H ** -0.5, 0.21875, ((1, 8),), jnp.float32)
    norm_params = jnp.clip(jax.random.uniform(splits[10], (2, 4, H), jnp.float32, 0.5, 1.5), 0.5, 1.5)
    latent_bias = normal_values(splits[11], (2, Z), 0.5, 3.0, (), jnp.float32)
    out_bias = normal_values(splits[12], (G,), 0.5, 3.0, ((0, 8),), jnp.float32)
    running_mean = normal_values(splits[13], (4, H), 0.5, 3.0, (), jnp.float32)
    running_variance = jnp.clip(jnp.exp(jax.random.uniform(splits[14], (4, H), jnp.float32, math.log(0.5), math.log(4.0))), 0.5, 4.0)
    mom_enc_in = normal_values(splits[15], (G, H), (2 * (CELLS / (G * H)) ** 0.5), 1.5, ((0, 8),), jnp.float32)
    mom_enc_mid = normal_values(splits[16], (H, H), ((CELLS / (G * H)) ** 0.5), 0.75, (), jnp.float32)
    mom_latent_w = normal_values(splits[17], (2, H, Z), ((CELLS / (G * Z)) ** 0.5), 2.0, (), jnp.float32)
    mom_dec_in = normal_values(splits[18], (Z, H), ((CELLS / (G * H)) ** 0.5), 0.75, (), jnp.float32)
    mom_dec_mid = normal_values(splits[19], (H, H), ((CELLS / (G * H)) ** 0.5), 0.75, (), jnp.float32)
    mom_dec_out = normal_values(splits[20], (H, G), (CELLS ** 0.5 / G), 0.5, ((1, 8),), jnp.float32)
    mom_norm = normal_values(splits[21], (2, 4, H), ((CELLS / (G * H)) ** 0.5), 0.75, (), jnp.float32)
    mom_latent_bias = normal_values(splits[22], (2, Z), ((CELLS / (G * Z)) ** 0.5), 2.0, (), jnp.float32)
    mom_out_bias = normal_values(splits[23], (G,), (2 * CELLS ** 0.5 / G), 1.0, ((0, 8),), jnp.float32)
    return {"counts": counts, "study": study, "study_gene_mask": study_gene_mask, "noise": noise, "enc_in": enc_in, "enc_mid": enc_mid, "latent_w": latent_w, "dec_in": dec_in, "dec_mid": dec_mid, "dec_out": dec_out, "norm_params": norm_params, "latent_bias": latent_bias, "out_bias": out_bias, "running_mean": running_mean, "running_variance": running_variance, "mom_enc_in": mom_enc_in, "mom_enc_mid": mom_enc_mid, "mom_latent_w": mom_latent_w, "mom_dec_in": mom_dec_in, "mom_dec_mid": mom_dec_mid, "mom_dec_out": mom_dec_out, "mom_norm": mom_norm, "mom_latent_bias": mom_latent_bias, "mom_out_bias": mom_out_bias}


@jax.custom_vjp
def low(v):
    return lax.optimization_barrier(v.astype(jnp.bfloat16)).astype(jnp.float32)

@jax.custom_vjp
def low_back(v):
    return v

def low_keep(v):
    return (low(v), None)

def low_pass(kept, grad):
    return (grad,)

def back_keep(v):
    return (v, None)

def back_low(kept, grad):
    return (low(grad),)
low.defvjp(low_keep, low_pass)
low_back.defvjp(back_keep, back_low)
EPSILON = 1e-05
ALPHA_KL = 5e-05
MOMENTUM = 0.95
RATE = 0.5
RATE_VECTOR = 0.2
COEF_A = 3.4445
COEF_B = -4.775
COEF_C = 2.0315
HIGH = lax.Precision.HIGHEST

def matmul(left, right):
    return jnp.dot(left, right, precision=HIGH, preferred_element_type=jnp.float32)

def batch_norm(values, norm_params, layer):
    batch_mean = lax.optimization_barrier(jnp.mean(values, axis=0))
    batch_var = lax.optimization_barrier(jnp.mean(values * values, axis=0)) - batch_mean * batch_mean
    scaled = (values - batch_mean) * lax.rsqrt(batch_var + EPSILON)
    shifted = scaled * norm_params[0, layer] + norm_params[1, layer]
    return (jax.nn.gelu(shifted), batch_mean, batch_var)

def forward(enc_in, enc_mid, latent_w, dec_in, dec_mid, dec_out, norm_params, latent_bias, out_bias, counts, gene_mask, noise):
    first = low_back(matmul(counts, low(enc_in)))
    hidden_one, mean_one, var_one = batch_norm(first, norm_params, 0)
    second = low_back(matmul(low(hidden_one), low(enc_mid)))
    hidden_two, mean_two, var_two = batch_norm(second, norm_params, 1)
    two_low = low(hidden_two)
    latent_mean = low_back(matmul(two_low, low(latent_w[0])) + latent_bias[0])
    latent_logvar = low_back(matmul(two_low, low(latent_w[1])) + latent_bias[1])
    sample = low(latent_mean + noise * jnp.exp(0.5 * latent_logvar))
    third = low_back(matmul(sample, low(dec_in)))
    hidden_three, mean_three, var_three = batch_norm(third, norm_params, 2)
    fourth = low_back(matmul(low(hidden_three), low(dec_mid)))
    hidden_four, mean_four, var_four = batch_norm(fourth, norm_params, 3)
    decoded = low_back(matmul(low(hidden_four), low(dec_out)) + out_bias)
    genes = counts.shape[1]
    error = decoded - counts
    total = 0.5 / genes * jnp.sum(gene_mask * error * error)
    total = total + ALPHA_KL / genes * 0.5 * jnp.sum(jnp.exp(latent_logvar) + latent_mean * latent_mean - 1.0 - latent_logvar)
    means = jnp.stack([mean_one, mean_two, mean_three, mean_four])
    variances = jnp.stack([var_one, var_two, var_three, var_four])
    return (total, (decoded, means, variances))

def orthogonal(moment):
    current = moment / (jnp.sqrt(jnp.sum(moment * moment)) + 1e-07)
    incoming_rows, cols_out = moment.shape
    for iteration in range(NS):
        if incoming_rows >= cols_out:
            gram = matmul(current.T, current)
            current = COEF_A * current + matmul(current, COEF_B * gram + COEF_C * matmul(gram, gram))
        else:
            gram = matmul(current, current.T)
            current = COEF_A * current + matmul(COEF_B * gram + COEF_C * matmul(gram, gram), current)
    return current

def muon(weight, moment, grad):
    new_moment = MOMENTUM * moment + grad
    factor = math.sqrt(max(1.0, weight.shape[1] / weight.shape[0]))
    return (weight - RATE * factor * orthogonal(new_moment), new_moment)

def vector_step(value, moment, grad):
    new_moment = MOMENTUM * moment + grad
    square = lax.optimization_barrier(jnp.mean(new_moment * new_moment, axis=-1, keepdims=True))
    return (value - RATE_VECTOR * new_moment * lax.rsqrt(square + 1e-06), new_moment)

def reference(counts, study, study_gene_mask, noise, enc_in, enc_mid, latent_w, dec_in, dec_mid, dec_out, norm_params, latent_bias, out_bias, running_mean, running_variance, mom_enc_in, mom_enc_mid, mom_latent_w, mom_dec_in, mom_dec_mid, mom_dec_out, mom_norm, mom_latent_bias, mom_out_bias):
    counts_wide = counts.astype(jnp.float32)
    gene_mask = study_gene_mask[study].astype(jnp.float32)
    params = (enc_in, enc_mid, latent_w, dec_in, dec_mid, dec_out, norm_params, latent_bias, out_bias)

    def objective(*values):
        return forward(*values, counts_wide, gene_mask, noise)
    total, pullback, extras = jax.vjp(objective, *params, has_aux=True)
    decoded, means, variances = extras
    grads = pullback(jnp.ones((), jnp.float32))
    cells = counts.shape[0]
    new_enc_in, new_mom_enc_in = muon(enc_in, mom_enc_in, grads[0])
    new_enc_mid, new_mom_enc_mid = muon(enc_mid, mom_enc_mid, grads[1])
    mean_w, mean_m = muon(latent_w[0], mom_latent_w[0], grads[2][0])
    var_w, var_m = muon(latent_w[1], mom_latent_w[1], grads[2][1])
    new_dec_in, new_mom_dec_in = muon(dec_in, mom_dec_in, grads[3])
    new_dec_mid, new_mom_dec_mid = muon(dec_mid, mom_dec_mid, grads[4])
    new_dec_out, new_mom_dec_out = muon(dec_out, mom_dec_out, grads[5])
    new_norm, new_mom_norm = vector_step(norm_params, mom_norm, grads[6])
    new_latent_bias, new_mom_latent_bias = vector_step(latent_bias, mom_latent_bias, grads[7])
    new_out_bias, new_mom_out_bias = vector_step(out_bias, mom_out_bias, grads[8])
    new_running_mean = 0.9 * running_mean + 0.1 * means
    updated_running_variance = 0.9 * running_variance + 0.1 * variances * (cells / (cells - 1.0))
    return (decoded.astype(jnp.bfloat16), total / cells, new_enc_in, new_mom_enc_in, new_enc_mid, new_mom_enc_mid, jnp.stack([mean_w, var_w]), jnp.stack([mean_m, var_m]), new_dec_in, new_mom_dec_in, new_dec_mid, new_mom_dec_mid, new_dec_out, new_mom_dec_out, new_norm, new_mom_norm, new_latent_bias, new_mom_latent_bias, new_out_bias, new_mom_out_bias, new_running_mean, updated_running_variance)
```

```python
import math

import jax
import jax.numpy as jnp
from jax import lax
from jax.experimental import pallas as pl
from jax.experimental.pallas import tpu as pltpu
from jax.sharding import PartitionSpec as P

NS = 5


EPSILON = 1e-05
ALPHA_KL = 5e-05
MOMENTUM = 0.95
RATE = 0.5
RATE_VECTOR = 0.2
COEF_A = 3.4445
COEF_B = -4.775
COEF_C = 2.0315


def inner_rows(left, right):
    return lax.dot_general(
        left, right, (((0,), (0,)), ((), ())), preferred_element_type=jnp.float32
    )


def outer_cols(left, right):
    return lax.dot_general(
        left, right, (((1,), (1,)), ((), ())), preferred_element_type=jnp.float32
    )


def rows_times(left, right):
    return jnp.dot(left, right, preferred_element_type=jnp.float32)


def low(values):
    return values.astype(jnp.bfloat16)


def pair_tree(values):
    while len(values) > 1:
        values = [values[at] + values[at + 1] for at in range(0, len(values), 2)]
    return values[0]


def swap(values, distance, axis):
    pairs = [(device, device ^ distance) for device in range(lax.axis_size(axis))]
    return lax.ppermute(values, axis, pairs)


def cell_sum(values):
    count = lax.axis_size("cell")
    if count & (count - 1):
        return lax.psum(values, "cell")
    return pair_tree(
        [values] + [swap(values, distance, "cell") for distance in range(1, count)]
    )


def cell_scatter(blocks):
    count = lax.axis_size("cell")
    me = lax.axis_index("cell")

    def block(owner):
        return lax.dynamic_index_in_dim(blocks, owner, 0, keepdims=False)

    return pair_tree(
        [block(me)]
        + [swap(block(me ^ distance), distance, "cell") for distance in range(1, count)]
    )


def gene_gather(values):
    count = lax.axis_size("gene")
    me = lax.axis_index("gene")
    gathered = jnp.zeros((count,) + values.shape, values.dtype)
    for distance in range(0, count, 2):
        near = values if distance == 0 else swap(values, distance, "gene")
        far = swap(near, 1, "gene")
        gathered = lax.dynamic_update_index_in_dim(gathered, near, me ^ distance, 0)
        gathered = lax.dynamic_update_index_in_dim(gathered, far, me ^ distance ^ 1, 0)
    return gathered.reshape((count * values.shape[0],) + values.shape[1:])


def scatter_pieces(pieces, moments):
    count = lax.axis_size("cell")
    width = pieces[0].shape[1]

    def pack(entries):
        blocks = [entry.reshape(count, -1, width) for entry in entries]
        rows = sum(block.shape[1] for block in blocks)
        blocks.append(jnp.zeros((count, -rows % 8, width), jnp.float32))
        return jnp.concatenate(blocks, axis=1)

    known = [
        jnp.zeros_like(piece) if moment is None else MOMENTUM * moment
        for piece, moment in zip(pieces, moments)
    ]
    known = lax.dynamic_index_in_dim(pack(known), lax.axis_index("cell"), 0, keepdims=False)
    return cell_scatter(pack(pieces)) + known


def join(values, distance, axis, at):
    other = swap(values, distance, axis)
    upper = (lax.axis_index(axis) & distance) != 0
    return jnp.stack(
        [jnp.where(upper, other, values), jnp.where(upper, values, other)], axis=at
    )


def spread(values, axis, at=0):
    shape = values.shape
    distance = lax.axis_size(axis) // 2
    place = at
    while distance:
        values = join(values, distance, axis, place)
        distance //= 2
        place += 1
    return values.reshape(shape[:at] + (lax.axis_size(axis),) + shape[at:])


def cell_total(values, kind=jnp.float32):
    count = lax.axis_size("cell")
    me = lax.axis_index("cell")
    distance = 1
    while distance < count:
        half = values.shape[0] // 2
        upper = ((me & distance) != 0).astype(jnp.int32)
        keep = lax.dynamic_slice_in_dim(values, upper * half, half, 0)
        give = lax.dynamic_slice_in_dim(values, (1 - upper) * half, half, 0)
        values = keep + swap(give, distance, "cell")
        distance *= 2
    if kind == jnp.bfloat16:
        values = low(lax.reduce_precision(values, 8, 7))
    while distance > 1:
        distance //= 2
        values = join(values, distance, "cell", 0).reshape(-1, values.shape[1])
    return values.astype(jnp.float32)


def by_core(mine):
    other = swap(mine, 1, "cell")
    odd = (lax.axis_index("cell") & 1) != 0
    return jnp.where(odd, other, mine), jnp.where(odd, mine, other)


def gather_pieces(block, heights):
    count = lax.axis_size("cell")
    gathered = lax.all_gather(block, ("gene", "cell"), axis=0, tiled=False)
    start = 0
    whole = []
    for height in heights:
        part = gathered[:, start : start + height // count]
        whole.append(part.reshape(-1, part.shape[2]))
        start += height // count
    return whole


def gather_slices(pieces, moments):
    slices = [
        cell_sum(piece) if moment is None else cell_sum(piece) + MOMENTUM * moment
        for piece, moment in zip(pieces, moments)
    ]
    return slices[:1] + [gather_rows(values, "gene") for values in slices[1:]]


def lengthen(values, axis, multiple):
    room = [(0, 0)] * values.ndim
    room[axis] = (0, -values.shape[axis] % multiple)
    return jnp.pad(values, room)


def three_parts(values):
    first = lax.reduce_precision(values, 8, 7)
    second = lax.reduce_precision(values - first, 8, 7)
    return low(jnp.stack([first, second, values - first - second], axis=1))


def gather_rows(values, axes):
    return lax.all_gather(values, axes, axis=0, tiled=True)


def rescale(values, batch_mean, inverse, norm_params, layer):
    scaled = (values - batch_mean) * inverse
    return scaled, scaled * norm_params[0, layer] + norm_params[1, layer]


def normalize(values, norm_params, layer, cells):
    totals = cell_sum(jnp.stack([jnp.sum(values, axis=0), jnp.sum(values * values, axis=0)]))
    batch_mean = totals[0] / cells
    batch_var = totals[1] / cells - batch_mean * batch_mean
    inverse = lax.rsqrt(batch_var + EPSILON)
    scaled, shifted = rescale(values, batch_mean, inverse, norm_params, layer)
    return (low(jax.nn.gelu(shifted)), (values, inverse, batch_mean, batch_var))


def norm_back(grad_out, saved, norm_params, layer, cells):
    values, inverse, batch_mean = lax.optimization_barrier(saved[:3])
    scaled, shifted = rescale(values, batch_mean, inverse, norm_params, layer)
    unused, pullback = jax.vjp(jax.nn.gelu, shifted)
    grad_shift = pullback(grad_out)[0]
    sums = cell_sum(jnp.stack([jnp.sum(grad_shift, axis=0), jnp.sum(grad_shift * scaled, axis=0)]))
    grad_in = (
        norm_params[0, layer] * inverse * (grad_shift - sums[0] / cells - scaled * sums[1] / cells)
    )
    return (low(grad_in), sums[1], sums[0])


def orthogonal_shared(own):
    total = lax.psum(jnp.sum(own * own), "gene")
    current = own / (jnp.sqrt(total) + 1e-07)
    for iteration in range(NS):
        operand = low(current)
        gram = lax.psum(inner_rows(operand, operand), "gene")
        gram_low = low(gram)
        polynom = low(COEF_B * gram + COEF_C * rows_times(gram_low, gram_low))
        current = COEF_A * current + rows_times(operand, polynom)
    return current


def iterate(operand, gram, gram_low, polynom, own=None, own_low=None):
    gram[...] = outer_cols(operand[...], operand[...])
    gram_low[...] = low(gram[...])
    square = rows_times(gram_low[...], gram_low[...])
    polynom[...] = low(COEF_B * gram[...] + COEF_C * square)
    if own is not None:
        own[...] = COEF_A * own[...] + rows_times(polynom[...], own_low[...])
        own_low[...] = low(own[...])


def square_kernel(place, even, odd, result, current, operand, gram, gram_low, polynom):
    def load(moment):
        values = moment[...]
        current[...] = values * (1.0 / (jnp.sqrt(jnp.sum(values * values)) + 1e-07))

    pl.when(place[0] == 0)(lambda: load(even))
    pl.when(place[0] != 0)(lambda: load(odd))

    def step(iteration, carry):
        operand[...] = low(current[...])
        iterate(operand, gram, gram_low, polynom)
        current[...] = COEF_A * current[...] + rows_times(polynom[...], operand[...])
        return carry

    lax.fori_loop(0, NS, step, 0)
    result[...] = low(current[...])


def tall_kernel(
    place, even, odd, result, current, operand, own, own_low, gram, gram_low, polynom
):
    rows = even.shape[0]
    tile = 256

    def load(moment):
        def add_square(at, total):
            values = moment[pl.ds(pl.multiple_of(at * tile, tile), tile), :].astype(jnp.float32)
            return total + jnp.sum(values * values)

        total = lax.fori_loop(0, rows // tile, add_square, jnp.float32(0))
        scale = 1.0 / (jnp.sqrt(total) + 1e-07)

        def turn(at, carry):
            here = pl.ds(pl.multiple_of(at * tile, tile), tile)
            values = moment[here, :].astype(jnp.float32).T * scale
            current[:, here] = values
            operand[:, here] = low(values)
            return carry

        lax.fori_loop(0, rows // tile, turn, 0)
        mine = pl.ds(pl.multiple_of(place[1], 16), own.shape[1])
        own[...] = moment[mine, :].astype(jnp.float32).T * scale
        own_low[...] = low(own[...])

    pl.when(place[0] == 0)(lambda: load(even))
    pl.when(place[0] != 0)(lambda: load(odd))

    def step(iteration, carry):
        iterate(operand, gram, gram_low, polynom, own, own_low)

        @pl.when(iteration < NS - 1)
        def _():
            current[...] = COEF_A * current[...] + rows_times(polynom[...], operand[...])
            operand[...] = low(current[...])

        return carry

    lax.fori_loop(0, NS, step, 0)
    result[...] = low(own[...].T)


def narrow_kernel(moments, results):
    for number in range(moments.shape[0]):
        values = moments[number]
        results[number] = values / (jnp.sqrt(jnp.sum(values * values)) + 1e-07)
    exact = dict(precision=lax.Precision.HIGHEST, preferred_element_type=jnp.float32)

    def step(iteration, carry):
        for number in range(moments.shape[0]):
            values = results[number]
            gram = lax.dot_general(values, values, (((1,), (1,)), ((), ())), **exact)
            polynom = COEF_B * gram + COEF_C * jnp.dot(gram, gram, **exact)
            results[number] = COEF_A * values + jnp.dot(polynom, values, **exact)
        return carry

    lax.fori_loop(0, NS, step, 0)


def on_chip(kernel, shape, scratch, flops, *operands):
    space = pl.BlockSpec(memory_space=pltpu.VMEM)
    scalars = pl.BlockSpec(memory_space=pltpu.SMEM)
    return pl.pallas_call(
        kernel,
        out_shape=shape,
        in_specs=[scalars if operand.dtype == jnp.int32 else space for operand in operands],
        out_specs=space,
        scratch_shapes=[pltpu.VMEM(*entry) for entry in scratch],
        compiler_params=pltpu.CompilerParams(vmem_limit_bytes=48 * 2**20),
        cost_estimate=pl.CostEstimate(flops=flops, bytes_accessed=2**22, transcendentals=0),
    )(*operands)


def pair_place():
    return (lax.axis_index("cell") & 1).astype(jnp.int32)


def orthogonal_squares(even, odd):
    width = even.shape[0]
    mine = on_chip(
        square_kernel,
        jax.ShapeDtypeStruct(even.shape, jnp.bfloat16),
        [
            ((width, width), jnp.float32),
            ((width, width), jnp.bfloat16),
            ((width, width), jnp.float32),
            ((width, width), jnp.bfloat16),
            ((width, width), jnp.bfloat16),
        ],
        6 * NS * width**3,
        pair_place()[None],
        even,
        odd,
    )
    return by_core(mine)


def orthogonal_talls(even, odd, own_rows):
    rows, width = even.shape
    start = (lax.axis_index("gene") * own_rows).astype(jnp.int32)
    mine = on_chip(
        tall_kernel,
        jax.ShapeDtypeStruct((own_rows, width), jnp.bfloat16),
        [
            ((width, rows), jnp.float32),
            ((width, rows), jnp.bfloat16),
            ((width, own_rows), jnp.float32),
            ((width, own_rows), jnp.bfloat16),
            ((width, width), jnp.float32),
            ((width, width), jnp.bfloat16),
            ((width, width), jnp.bfloat16),
        ],
        2 * NS * width * width * (2 * rows + width),
        jnp.stack([pair_place(), start]),
        even,
        odd,
    )
    return by_core(mine)


def orthogonal_narrow(moments):
    count, width, length = moments.shape
    return on_chip(
        narrow_kernel,
        jax.ShapeDtypeStruct(moments.shape, jnp.float32),
        [],
        12 * NS * count * width * width * (2 * length + width),
        moments,
    )


def vector_step(value, moment, square):
    return value - RATE_VECTOR * moment * lax.rsqrt(square + 1e-06)


def shards(
    counts,
    study,
    study_gene_mask,
    noise,
    enc_in,
    enc_mid,
    latent_w,
    dec_in,
    dec_mid,
    dec_out,
    norm_params,
    latent_bias,
    out_bias,
    running_mean,
    running_variance,
    mom_enc_in,
    mom_enc_mid,
    mom_latent_w,
    mom_dec_in,
    mom_dec_mid,
    mom_dec_out,
    mom_norm,
    mom_latent_bias,
    mom_out_bias,
):
    gene_count = lax.axis_size("gene")
    cell_count = lax.axis_size("cell")
    gene_at = lax.axis_index("gene")
    cell_at = lax.axis_index("cell")
    group_rows, gene_local = counts.shape
    cells = group_rows * cell_count
    genes = gene_local * gene_count
    hidden_width = enc_mid.shape[0]
    latent_width = dec_in.shape[0]
    study_labels = study_gene_mask.shape[0]
    devices = gene_count * cell_count
    whole = (
        group_rows * genes <= 2**22
        and genes * hidden_width <= 2**21
        and genes % 256 == 0
        and hidden_width % devices == 0
        and gene_local % (8 * cell_count) == 0
        and devices & (devices - 1) == 0
    )

    def own_rows(values, rows=gene_local):
        return lax.dynamic_slice_in_dim(values, gene_at * rows, rows, 0)

    selection = low(study[None, :] == jnp.arange(study_labels, dtype=jnp.int32)[:, None])
    enc_in_low = low(enc_in)
    enc_mid_low = low(enc_mid)
    latent_low = low(latent_w)
    dec_in_low = low(dec_in)
    dec_mid_low = low(dec_mid)
    dec_out_low = low(dec_out)
    counts_turned = counts.T
    last_layer = jnp.concatenate(
        [dec_out_low.T, low(study_gene_mask.T), three_parts(out_bias)], axis=1
    )
    if whole:
        part = gene_local // cell_count

        def own_part(values):
            return lax.dynamic_slice_in_dim(values, cell_at * part, part, 0)

        counts_turned = gene_gather(counts_turned)
        enc_in_low = spread(spread(own_part(enc_in_low), "gene"), "cell", 1)
        enc_in_low = enc_in_low.reshape(genes, hidden_width)
        first = inner_rows(counts_turned, enc_in_low)
        all_noise = spread(noise, "gene").reshape(group_rows, latent_width)
        last_layer = gather_rows(own_part(last_layer), ("gene", "cell"))
    else:
        first = lax.psum(inner_rows(counts_turned, enc_in_low), "gene")
        all_noise = gather_rows(noise, "gene")
    dec_out_turned = last_layer[:, :hidden_width]
    mask_turned = last_layer[:, hidden_width : hidden_width + study_labels]
    bias_column = jnp.sum(
        last_layer[:, hidden_width + study_labels :].astype(jnp.float32), axis=1, keepdims=True
    )
    one_low, saved_one = normalize(first, norm_params, 0, cells)
    second = rows_times(one_low, enc_mid_low)
    two_low, saved_two = normalize(second, norm_params, 1, cells)
    latent_mean = rows_times(two_low, latent_low[0]) + latent_bias[0]
    latent_logvar = rows_times(two_low, latent_low[1]) + latent_bias[1]
    spread_factor = jnp.exp(0.5 * latent_logvar)
    sample_low = low(latent_mean + all_noise * spread_factor)
    third = rows_times(sample_low, dec_in_low)
    three_low, saved_three = normalize(third, norm_params, 2, cells)
    fourth = rows_times(three_low, dec_mid_low)
    four_low, saved_four = normalize(fourth, norm_params, 3, cells)
    decoded = outer_cols(dec_out_turned, four_low) + bias_column
    error = decoded - counts_turned.astype(jnp.float32)
    gene_mask = rows_times(mask_turned, selection)
    loss_part = 0.5 / genes * jnp.sum(gene_mask * error * error)
    grad_decoded = low(gene_mask * error / genes)
    grad_four = inner_rows(grad_decoded, dec_out_turned)
    if whole:
        own_grad = own_rows(grad_decoded)
    else:
        loss_part, grad_four = lax.psum((loss_part, grad_four), "gene")
        own_grad = grad_decoded
    recon = low(rows_times(four_low, dec_out_low) + out_bias)
    kl_scale = ALPHA_KL / genes
    loss_part = loss_part + kl_scale * 0.5 * jnp.sum(
        jnp.exp(latent_logvar) + latent_mean * latent_mean - 1.0 - latent_logvar
    )
    grad_dec_out = rows_times(own_grad, four_low)
    grad_out_bias = jnp.sum(own_grad, axis=1, dtype=jnp.float32)

    def bias_rows(values):
        return lengthen(values.reshape(cell_count, -1), 1, hidden_width)

    pieces = [grad_dec_out, bias_rows(grad_out_bias)]
    moments = [mom_dec_out.T, bias_rows(mom_out_bias)]
    if whole:
        decoder = scatter_pieces(pieces, moments)
    else:
        own_moment_out, moment_bias = gather_slices(pieces, moments)
    grad_a4, gain_four, shift_four = norm_back(grad_four, saved_four, norm_params, 3, cells)
    grad_dec_mid = cell_total(inner_rows(three_low, grad_a4), jnp.bfloat16)
    grad_three = outer_cols(grad_a4, dec_mid_low)
    grad_a3, gain_three, shift_three = norm_back(grad_three, saved_three, norm_params, 2, cells)
    if whole:
        decoder, grad_a3 = lax.optimization_barrier((decoder, grad_a3))
        moment_out, moment_bias = gather_pieces(decoder, [gene_local, cell_count])
        own_moment_out = own_rows(moment_out)
    grad_dec_in = inner_rows(sample_low, grad_a3)
    grad_sample = outer_cols(grad_a3, dec_in_low)
    grad_mean = low(grad_sample + kl_scale * latent_mean)
    grad_logvar = low(
        grad_sample * all_noise * 0.5 * spread_factor
        + kl_scale * 0.5 * (jnp.exp(latent_logvar) - 1.0)
    )
    grad_pair = jnp.concatenate([grad_mean, grad_logvar], axis=1)
    latent_pair = jnp.concatenate([latent_low[0], latent_low[1]], axis=1)
    grad_narrow = jnp.concatenate([inner_rows(grad_pair, two_low), grad_dec_in])
    grad_narrow = cell_total(lengthen(grad_narrow, 0, 8 * cell_count))
    small = cell_sum(
        jnp.concatenate([jnp.sum(grad_pair, axis=0, dtype=jnp.float32), loss_part[None]])
    )
    grad_two = outer_cols(grad_pair, latent_pair)
    grad_a2, gain_two, shift_two = norm_back(grad_two, saved_two, norm_params, 1, cells)
    grad_enc_mid = cell_total(inner_rows(one_low, grad_a2), jnp.bfloat16)
    grad_one = outer_cols(grad_a2, enc_mid_low)
    grad_a1, gain_one, shift_one = norm_back(grad_one, saved_one, norm_params, 0, cells)
    grad_enc_in = inner_rows(counts, grad_a1)
    if whole:
        encoder = scatter_pieces([grad_enc_in], [mom_enc_in])
        moment_first = gather_pieces(low(encoder), [gene_local])[0]
        new_mom_enc_in = own_rows(moment_first).astype(jnp.float32)
    else:
        new_mom_enc_in = MOMENTUM * mom_enc_in + cell_sum(grad_enc_in)
    new_mom_dec_out = own_moment_out.T

    grad_latent_bias = small[: 2 * latent_width].reshape(2, latent_width)
    total = small[2 * latent_width]
    moment_bias = moment_bias[:, : gene_local // cell_count].reshape(gene_count, gene_local)
    new_mom_out_bias = lax.dynamic_index_in_dim(moment_bias, gene_at, 0, keepdims=False)
    new_out_bias = vector_step(out_bias, new_mom_out_bias, jnp.mean(moment_bias * moment_bias))

    new_mom_dec_mid = MOMENTUM * mom_dec_mid + grad_dec_mid
    new_mom_enc_mid = MOMENTUM * mom_enc_mid + grad_enc_mid
    turned_enc_mid, turned_dec_mid = orthogonal_squares(new_mom_enc_mid, new_mom_dec_mid)
    new_enc_mid = enc_mid - RATE * turned_enc_mid.astype(jnp.float32)
    new_dec_mid = dec_mid - RATE * turned_dec_mid.astype(jnp.float32)

    grad_latent = grad_narrow[: 2 * latent_width].reshape(2, latent_width, hidden_width)
    grad_dec_in = grad_narrow[2 * latent_width : 3 * latent_width]
    new_mom_dec_in = MOMENTUM * mom_dec_in + grad_dec_in
    turned_latent = MOMENTUM * jnp.swapaxes(mom_latent_w, 1, 2) + grad_latent
    new_mom_latent_w = jnp.swapaxes(turned_latent, 1, 2)
    narrow = orthogonal_narrow(jnp.concatenate([turned_latent, new_mom_dec_in[None]]))
    factor = math.sqrt(max(1.0, hidden_width / latent_width))
    new_dec_in = dec_in - RATE * factor * narrow[2]
    new_latent_w = latent_w - RATE * jnp.swapaxes(narrow[:2], 1, 2)

    if whole:
        turned_in, turned_out = orthogonal_talls(moment_first, moment_out, gene_local)
    else:
        turned_in = orthogonal_shared(new_mom_enc_in)
        turned_out = orthogonal_shared(own_moment_out)
    new_enc_in = enc_in - RATE * turned_in.astype(jnp.float32)
    factor = math.sqrt(max(1.0, genes / hidden_width))
    new_dec_out = dec_out - RATE * factor * turned_out.astype(jnp.float32).T

    grad_norm = jnp.stack(
        [
            jnp.stack([gain_one, gain_two, gain_three, gain_four]),
            jnp.stack([shift_one, shift_two, shift_three, shift_four]),
        ]
    )
    new_mom_norm = MOMENTUM * mom_norm + grad_norm
    new_norm = vector_step(
        norm_params, new_mom_norm, jnp.mean(new_mom_norm * new_mom_norm, axis=-1, keepdims=True)
    )
    new_mom_latent_bias = MOMENTUM * mom_latent_bias + grad_latent_bias
    new_latent_bias = vector_step(
        latent_bias,
        new_mom_latent_bias,
        jnp.mean(new_mom_latent_bias * new_mom_latent_bias, axis=-1, keepdims=True),
    )
    means = jnp.stack([saved_one[2], saved_two[2], saved_three[2], saved_four[2]])
    variances = jnp.stack([saved_one[3], saved_two[3], saved_three[3], saved_four[3]])
    new_running_mean = 0.9 * running_mean + 0.1 * means
    updated_running_variance = 0.9 * running_variance + 0.1 * variances * (cells / (cells - 1.0))
    return (
        recon,
        total / cells,
        new_enc_in,
        new_mom_enc_in,
        new_enc_mid,
        new_mom_enc_mid,
        new_latent_w,
        new_mom_latent_w,
        new_dec_in,
        new_mom_dec_in,
        new_dec_mid,
        new_mom_dec_mid,
        new_dec_out,
        new_mom_dec_out,
        new_norm,
        new_mom_norm,
        new_latent_bias,
        new_mom_latent_bias,
        new_out_bias,
        new_mom_out_bias,
        new_running_mean,
        updated_running_variance,
    )


def solution(mesh):
    in_specs = (
        P("cell", "gene"),
        P("cell"),
        P(None, "gene"),
        P(("cell", "gene"), None),
        P("gene", None),
        P(),
        P(),
        P(),
        P(),
        P(None, "gene"),
        P(),
        P(),
        P("gene"),
        P(),
        P(),
        P("gene", None),
        P(),
        P(),
        P(),
        P(),
        P(None, "gene"),
        P(),
        P(),
        P("gene"),
    )
    out_specs = (
        P("cell", "gene"),
        P(),
        P("gene", None),
        P("gene", None),
        P(),
        P(),
        P(),
        P(),
        P(),
        P(),
        P(),
        P(),
        P(None, "gene"),
        P(None, "gene"),
        P(),
        P(),
        P(),
        P(),
        P("gene"),
        P("gene"),
        P(),
        P(),
    )
    return jax.shard_map(shards, mesh=mesh, in_specs=in_specs, out_specs=out_specs, check_vma=False)
```

```python
import math

import jax
import jax.numpy as jnp
from jax import lax
from jax.experimental import pallas as pl
from jax.experimental.pallas import tpu as pltpu
from jax.sharding import PartitionSpec as P

NS = 5


EPSILON = 1e-05
ALPHA_KL = 5e-05
MOMENTUM = 0.95
RATE = 0.5
RATE_VECTOR = 0.2
COEF_A = 3.4445
COEF_B = -4.775
COEF_C = 2.0315


def inner_rows(left, right):
    return lax.dot_general(
        left, right, (((0,), (0,)), ((), ())), preferred_element_type=jnp.float32
    )


def outer_cols(left, right):
    return lax.dot_general(
        left, right, (((1,), (1,)), ((), ())), preferred_element_type=jnp.float32
    )


def rows_times(left, right):
    return jnp.dot(left, right, preferred_element_type=jnp.float32)


def low(values):
    return values.astype(jnp.bfloat16)


def pair_tree(values):
    while len(values) > 1:
        values = [values[at] + values[at + 1] for at in range(0, len(values), 2)]
    return values[0]


def swap(values, distance, axis):
    pairs = [(device, device ^ distance) for device in range(lax.axis_size(axis))]
    return lax.ppermute(values, axis, pairs)


def cell_sum(values):
    count = lax.axis_size("cell")
    if count & (count - 1):
        return lax.psum(values, "cell")
    return pair_tree(
        [values] + [swap(values, distance, "cell") for distance in range(1, count)]
    )


def cell_scatter(blocks):
    count = lax.axis_size("cell")
    me = lax.axis_index("cell")

    def block(owner):
        return lax.dynamic_index_in_dim(blocks, owner, 0, keepdims=False)

    return pair_tree(
        [block(me)]
        + [swap(block(me ^ distance), distance, "cell") for distance in range(1, count)]
    )


def first_gather(counts_turned, share, noise):
    count = lax.axis_size("gene")
    me = lax.axis_index("gene")
    even = (me & 1) == 0
    ring = [(device, (device + 2) % count) for device in range(count)]
    steps = count // 2
    height, width = counts_turned.shape
    rows, depth = share.shape
    near = jnp.concatenate([counts_turned, lengthen(share, 1, width)])
    whole = jnp.zeros((count, height, width), counts_turned.dtype)
    shares = jnp.zeros((count, 4, rows, depth), share.dtype)
    at_x, at_core = {}, {}
    distance, noise_place, noise_shape = count // 2, 0, noise.shape
    for step in range(steps + 2):
        moves = {}
        if distance:
            moves["noise"] = join(noise, distance, "gene", noise_place)
        if step < steps:
            moves["far"] = swap(near, 1, "gene")
        if step < steps - 1:
            moves["near"] = lax.ppermute(near, "gene", ring)
        if step - 1 in at_x:
            moves["x"] = join(at_x[step - 1], 2, "cell", 1)
        if step - 2 in at_core:
            moves["core"] = join(at_core[step - 2], 1, "cell", 2)
        moves = lax.optimization_barrier(moves)
        if distance:
            noise = moves["noise"]
            distance //= 2
            noise_place += 1
        if step < steps:
            source = (me + count - 2 * step) % count
            far = moves["far"]
            whole = lax.dynamic_update_index_in_dim(whole, near[:height], source, 0)
            whole = lax.dynamic_update_index_in_dim(whole, far[:height], source ^ 1, 0)
            own, other = near[height:, :depth], far[height:, :depth]
            at_x[step] = jnp.stack([jnp.where(even, own, other), jnp.where(even, other, own)])
        if step < steps - 1:
            near = moves["near"]
        if "x" in moves:
            at_core[step - 1] = moves["x"]
        if "core" in moves:
            base = (me + count - 2 * (step - 2)) % count - (me & 1)
            shares = lax.dynamic_update_slice(
                shares, moves["core"].reshape(2, 4, rows, depth), (base, 0, 0, 0)
            )
    return (
        whole.reshape(count * height, width),
        shares.reshape(-1, depth),
        noise.reshape(count * noise_shape[0], noise_shape[1]),
    )


def scatter_pieces(pieces, moments):
    count = lax.axis_size("cell")
    width = pieces[0].shape[1]

    def pack(entries):
        blocks = [entry.reshape(count, -1, width) for entry in entries]
        rows = sum(block.shape[1] for block in blocks)
        blocks.append(jnp.zeros((count, -rows % 8, width), jnp.float32))
        return jnp.concatenate(blocks, axis=1)

    known = [
        jnp.zeros_like(piece) if moment is None else MOMENTUM * moment
        for piece, moment in zip(pieces, moments)
    ]
    known = lax.dynamic_index_in_dim(pack(known), lax.axis_index("cell"), 0, keepdims=False)
    return cell_scatter(pack(pieces)) + known


def join(values, distance, axis, at):
    other = swap(values, distance, axis)
    upper = (lax.axis_index(axis) & distance) != 0
    return jnp.stack(
        [jnp.where(upper, other, values), jnp.where(upper, values, other)], axis=at
    )


def spread(values, axis, at=0):
    shape = values.shape
    distance = lax.axis_size(axis) // 2
    place = at
    while distance:
        values = join(values, distance, axis, place)
        distance //= 2
        place += 1
    return values.reshape(shape[:at] + (lax.axis_size(axis),) + shape[at:])


def cell_total(values):
    count = lax.axis_size("cell")
    distance = 1
    while distance < count:
        values = halve(values, distance)
        distance *= 2
    while distance > 1:
        distance //= 2
        values = unite(values, distance)
    return values


def by_core(mine):
    other = swap(mine, 1, "cell")
    odd = (lax.axis_index("cell") & 1) != 0
    return jnp.where(odd, other, mine), jnp.where(odd, mine, other)


def halve(values, distance, kind=jnp.float32):
    half = values.shape[0] // 2
    upper = ((lax.axis_index("cell") & distance) != 0).astype(jnp.int32)
    keep = lax.dynamic_slice_in_dim(values, upper * half, half, 0)
    give = lax.dynamic_slice_in_dim(values, (1 - upper) * half, half, 0)
    return keep + swap(give.astype(kind), distance, "cell").astype(jnp.float32)


def unite(values, distance):
    return join(values, distance, "cell", 0).reshape(-1, values.shape[1])


def rounded(values):
    return low(lax.reduce_precision(values, 8, 7))


def gather_block(block):
    return lax.all_gather(block, ("gene", "cell"), axis=0, tiled=False)


def cut_pieces(gathered, heights):
    count = lax.axis_size("cell")
    start = 0
    whole = []
    for height in heights:
        part = gathered[:, start : start + height // count]
        whole.append(part.reshape(-1, part.shape[2]))
        start += height // count
    return whole


def gather_slices(pieces, moments):
    slices = [
        cell_sum(piece) if moment is None else cell_sum(piece) + MOMENTUM * moment
        for piece, moment in zip(pieces, moments)
    ]
    return slices[:1] + [gather_rows(values, "gene") for values in slices[1:]]


def lengthen(values, axis, multiple):
    room = [(0, 0)] * values.ndim
    room[axis] = (0, -values.shape[axis] % multiple)
    return jnp.pad(values, room)


def three_parts(values):
    first = lax.reduce_precision(values, 8, 7)
    second = lax.reduce_precision(values - first, 8, 7)
    return low(jnp.stack([first, second, values - first - second], axis=1))


def gather_rows(values, axes):
    return lax.all_gather(values, axes, axis=0, tiled=True)


def rescale(values, batch_mean, inverse, norm_params, layer):
    scaled = (values - batch_mean) * inverse
    return scaled, scaled * norm_params[0, layer] + norm_params[1, layer]


def normalize(values, norm_params, layer, cells):
    totals = cell_sum(jnp.stack([jnp.sum(values, axis=0), jnp.sum(values * values, axis=0)]))
    batch_mean = totals[0] / cells
    batch_var = totals[1] / cells - batch_mean * batch_mean
    inverse = lax.rsqrt(batch_var + EPSILON)
    scaled, shifted = rescale(values, batch_mean, inverse, norm_params, layer)
    return (low(jax.nn.gelu(shifted)), (values, inverse, batch_mean, batch_var))


def norm_back(grad_out, saved, norm_params, layer, cells):
    values, inverse, batch_mean = lax.optimization_barrier(saved[:3])
    scaled, shifted = rescale(values, batch_mean, inverse, norm_params, layer)
    unused, pullback = jax.vjp(jax.nn.gelu, shifted)
    grad_shift = pullback(grad_out)[0]
    sums = cell_sum(jnp.stack([jnp.sum(grad_shift, axis=0), jnp.sum(grad_shift * scaled, axis=0)]))
    grad_in = (
        norm_params[0, layer] * inverse * (grad_shift - sums[0] / cells - scaled * sums[1] / cells)
    )
    return (low(grad_in), sums[1], sums[0])


def orthogonal_shared(own, axes="gene"):
    total = lax.psum(jnp.sum(own * own), axes)
    current = own / (jnp.sqrt(total) + 1e-07)
    for iteration in range(NS):
        operand = low(current)
        gram = lax.psum(inner_rows(operand, operand), axes)
        gram_low = low(gram)
        polynom = low(COEF_B * gram + COEF_C * rows_times(gram_low, gram_low))
        current = COEF_A * current + rows_times(operand, polynom)
    return current


def iterate(operand, gram, gram_low, polynom):
    gram[...] = outer_cols(operand, operand)
    gram_low[...] = low(gram[...])
    square = rows_times(gram_low[...], gram_low[...])
    polynom[...] = low(COEF_B * gram[...] + COEF_C * square)


def square_kernel(middle, square, current, operand, gram, gram_low, polynom):
    values = middle[...]
    current[...] = values * (1.0 / (jnp.sqrt(jnp.sum(values * values)) + 1e-07))

    def step(iteration, carry):
        operand[...] = low(current[...])
        iterate(operand[...], gram, gram_low, polynom)
        current[...] = COEF_A * current[...] + rows_times(polynom[...], operand[...])
        return carry

    lax.fori_loop(0, NS, step, 0)
    square[...] = low(current[...])


def tall_kernel(
    place, even, odd, tall, current, operand, own, own_low, gram, gram_low, polynom
):
    rows = even.shape[0]
    tile = 256

    def load(moment):
        def turn(at, total):
            here = pl.ds(pl.multiple_of(at * tile, tile), tile)
            values = moment[here, :].astype(jnp.float32)
            current[:, here] = values.T
            return total + jnp.sum(values * values)

        total = lax.fori_loop(0, rows // tile, turn, jnp.float32(0))
        scale = 1.0 / (jnp.sqrt(total) + 1e-07)

        def settle(at, carry):
            here = pl.ds(pl.multiple_of(at * tile, tile), tile)
            values = current[:, here] * scale
            current[:, here] = values
            operand[:, here] = low(values)
            return carry

        lax.fori_loop(0, rows // tile, settle, 0)
        mine = pl.ds(pl.multiple_of(place[1], 16), own.shape[1])
        own[...] = moment[mine, :].astype(jnp.float32).T * scale
        own_low[...] = low(own[...])

    pl.when(place[0] == 0)(lambda: load(even))
    pl.when(place[0] != 0)(lambda: load(odd))

    def step(iteration, carry):
        iterate(operand[...], gram, gram_low, polynom)
        own[...] = COEF_A * own[...] + rows_times(polynom[...], own_low[...])
        own_low[...] = low(own[...])

        @pl.when(iteration < NS - 1)
        def _():
            current[...] = COEF_A * current[...] + rows_times(polynom[...], operand[...])
            operand[...] = low(current[...])

        return carry

    lax.fori_loop(0, NS, step, 0)
    tall[...] = low(own[...].T)


def two_parts(values):
    first = low(values)
    return first, low(values - first.astype(jnp.float32))


def narrow_kernel(moments, results):
    count, rows = moments.shape[:2]

    def halves(values):
        return values[:rows] + values[rows:]

    def quarters(values):
        return halves(values[:, :rows] + values[:, rows:])

    for number in range(count):
        values = moments[number]
        results[number] = values * (1.0 / (jnp.sqrt(jnp.sum(values * values)) + 1e-07))

    def step(iteration, carry):
        for number in range(count):
            values = results[number]
            first, second = two_parts(values)
            stacked = jnp.concatenate([first, second], axis=0)
            gram = quarters(outer_cols(stacked, stacked))
            parts = two_parts(gram)
            square = quarters(
                rows_times(jnp.concatenate(parts, axis=0), jnp.concatenate(parts, axis=1))
            )
            parts = two_parts(COEF_B * gram + COEF_C * square)
            change = halves(rows_times(jnp.concatenate(parts, axis=0), first))
            results[number] = COEF_A * values + change + rows_times(parts[0], second)
        return carry

    lax.fori_loop(0, NS, step, 0)


def on_chip(kernel, shape, scratch, flops, *operands):
    space = pl.BlockSpec(memory_space=pltpu.VMEM)
    scalars = pl.BlockSpec(memory_space=pltpu.SMEM)
    return pl.pallas_call(
        kernel,
        out_shape=shape,
        in_specs=[scalars if operand.dtype == jnp.int32 else space for operand in operands],
        out_specs=jax.tree.map(lambda entry: space, shape),
        scratch_shapes=[pltpu.VMEM(*entry) for entry in scratch],
        compiler_params=pltpu.CompilerParams(vmem_limit_bytes=52 * 2**20),
        cost_estimate=pl.CostEstimate(flops=flops, bytes_accessed=2**22, transcendentals=0),
    )(*operands)


def orthogonal_squares(even, odd):
    width = even.shape[0]
    return on_chip(
        square_kernel,
        jax.ShapeDtypeStruct(even.shape, jnp.bfloat16),
        [
            ((width, width), jnp.float32),
            ((width, width), jnp.bfloat16),
            ((width, width), jnp.float32),
            ((width, width), jnp.bfloat16),
            ((width, width), jnp.bfloat16),
        ],
        6 * NS * width**3,
        jnp.where((lax.axis_index("cell") & 1) != 0, odd, even),
    )


def orthogonal_talls(even, odd, own_rows):
    rows, width = even.shape
    place = [lax.axis_index("cell") & 1, lax.axis_index("gene") * own_rows]
    return on_chip(
        tall_kernel,
        jax.ShapeDtypeStruct((own_rows, width), jnp.bfloat16),
        [
            ((width, rows), jnp.float32),
            ((width, rows), jnp.bfloat16),
            ((width, own_rows), jnp.float32),
            ((width, own_rows), jnp.bfloat16),
            ((width, width), jnp.float32),
            ((width, width), jnp.bfloat16),
            ((width, width), jnp.bfloat16),
        ],
        2 * NS * width * width * (2 * rows + width),
        jnp.stack(place).astype(jnp.int32),
        even,
        odd,
    )


def orthogonal_narrow(moments):
    count, width, length = moments.shape
    padded = lengthen(moments, 1, 128)
    return on_chip(
        narrow_kernel,
        jax.ShapeDtypeStruct(padded.shape, jnp.float32),
        [],
        8 * NS * count * padded.shape[1] ** 2 * (2 * length + padded.shape[1]),
        padded,
    )[:, :width]


def vector_step(value, moment, square):
    return value - RATE_VECTOR * moment * lax.rsqrt(square + 1e-06)


def shards(
    counts,
    study,
    study_gene_mask,
    noise,
    enc_in,
    enc_mid,
    latent_w,
    dec_in,
    dec_mid,
    dec_out,
    norm_params,
    latent_bias,
    out_bias,
    running_mean,
    running_variance,
    mom_enc_in,
    mom_enc_mid,
    mom_latent_w,
    mom_dec_in,
    mom_dec_mid,
    mom_dec_out,
    mom_norm,
    mom_latent_bias,
    mom_out_bias,
):
    gene_count = lax.axis_size("gene")
    cell_count = lax.axis_size("cell")
    gene_at = lax.axis_index("gene")
    cell_at = lax.axis_index("cell")
    group_rows, gene_local = counts.shape
    cells = group_rows * cell_count
    genes = gene_local * gene_count
    hidden_width = enc_mid.shape[0]
    latent_width = dec_in.shape[0]
    study_labels = study_gene_mask.shape[0]
    devices = gene_count * cell_count
    whole = (
        group_rows * genes <= 2**22
        and genes * hidden_width <= 2**21
        and genes % 256 == 0
        and hidden_width % devices == 0
        and gene_local % (8 * cell_count) == 0
        and devices & (devices - 1) == 0
        and cell_count == 4
    )

    def own_rows(values, rows=gene_local):
        return lax.dynamic_slice_in_dim(values, gene_at * rows, rows, 0)

    selection = low(study[None, :] == jnp.arange(study_labels, dtype=jnp.int32)[:, None])
    enc_in_low = low(enc_in)
    enc_mid_low = low(enc_mid)
    latent_low = low(latent_w)
    dec_in_low = low(dec_in)
    dec_mid_low = low(dec_mid)
    dec_out_low = low(dec_out)
    counts_turned = counts.T
    last_layer = jnp.concatenate(
        [dec_out_low.T, low(study_gene_mask.T), three_parts(out_bias)], axis=1
    )
    if whole:
        part = gene_local // cell_count

        def own_part(values):
            return lax.dynamic_slice_in_dim(values, cell_at * part, part, 0)

        counts_turned, enc_in_low, all_noise = first_gather(
            counts_turned, own_part(enc_in_low), noise
        )
        last_layer = own_part(last_layer)
        counts_turned, last_layer = lax.optimization_barrier((counts_turned, last_layer))
        first = inner_rows(counts_turned, enc_in_low)
        last_layer = gather_rows(last_layer, ("gene", "cell"))
    else:
        first = lax.psum(inner_rows(counts_turned, enc_in_low), "gene")
        all_noise = gather_rows(noise, "gene")
    dec_out_turned = last_layer[:, :hidden_width]
    mask_turned = last_layer[:, hidden_width : hidden_width + study_labels]
    bias_column = jnp.sum(
        last_layer[:, hidden_width + study_labels :].astype(jnp.float32), axis=1, keepdims=True
    )
    one_low, saved_one = normalize(first, norm_params, 0, cells)
    second = rows_times(one_low, enc_mid_low)
    two_low, saved_two = normalize(second, norm_params, 1, cells)
    latent_mean = rows_times(two_low, latent_low[0]) + latent_bias[0]
    latent_logvar = rows_times(two_low, latent_low[1]) + latent_bias[1]
    spread_factor = jnp.exp(0.5 * latent_logvar)
    sample_low = low(latent_mean + all_noise * spread_factor)
    third = rows_times(sample_low, dec_in_low)
    three_low, saved_three = normalize(third, norm_params, 2, cells)
    fourth = rows_times(three_low, dec_mid_low)
    four_low, saved_four = normalize(fourth, norm_params, 3, cells)
    decoded = outer_cols(dec_out_turned, four_low) + bias_column
    error = decoded - counts_turned.astype(jnp.float32)
    gene_mask = rows_times(mask_turned, selection)
    loss_part = 0.5 / genes * jnp.sum(gene_mask * error * error)
    grad_decoded = low(gene_mask * error / genes)
    grad_four = inner_rows(grad_decoded, dec_out_turned)
    if whole:
        own_grad = own_rows(grad_decoded)
    else:
        loss_part, grad_four = lax.psum((loss_part, grad_four), "gene")
        own_grad = grad_decoded
    recon = low(rows_times(four_low, dec_out_low) + out_bias)
    kl_scale = ALPHA_KL / genes
    loss_part = loss_part + kl_scale * 0.5 * jnp.sum(
        jnp.exp(latent_logvar) + latent_mean * latent_mean - 1.0 - latent_logvar
    )
    grad_dec_out = rows_times(own_grad, four_low)
    grad_out_bias = jnp.sum(own_grad, axis=1, dtype=jnp.float32)

    def bias_rows(values):
        return lengthen(values.reshape(cell_count, -1), 1, hidden_width)

    pieces = [grad_dec_out, bias_rows(grad_out_bias)]
    moments = [mom_dec_out.T, bias_rows(mom_out_bias)]
    if whole:
        decoder = scatter_pieces(pieces, moments)
    else:
        own_moment_out, moment_bias = gather_slices(pieces, moments)
    grad_a4, gain_four, shift_four = norm_back(grad_four, saved_four, norm_params, 3, cells)
    together = lax.optimization_barrier
    half = jnp.bfloat16
    grad_dec_mid = inner_rows(three_low, grad_a4)
    grad_three = outer_cols(grad_a4, dec_mid_low)
    if whole:
        grad_three, grad_dec_mid, decoder = together((grad_three, grad_dec_mid, decoder))
        decoder = gather_block(decoder)
        grad_dec_mid = halve(grad_dec_mid, 1, half)
    grad_a3, gain_three, shift_three = norm_back(grad_three, saved_three, norm_params, 2, cells)
    grad_dec_in = inner_rows(sample_low, grad_a3)
    grad_sample = outer_cols(grad_a3, dec_in_low)
    grad_mean = low(grad_sample + kl_scale * latent_mean)
    grad_logvar = low(
        grad_sample * all_noise * 0.5 * spread_factor
        + kl_scale * 0.5 * (jnp.exp(latent_logvar) - 1.0)
    )
    grad_pair = jnp.concatenate([grad_mean, grad_logvar], axis=1)
    latent_pair = jnp.concatenate([latent_low[0], latent_low[1]], axis=1)
    grad_narrow = jnp.concatenate([inner_rows(grad_pair, two_low), grad_dec_in])
    grad_narrow = lengthen(grad_narrow, 0, 8 * cell_count)
    small = jnp.concatenate([jnp.sum(grad_pair, axis=0, dtype=jnp.float32), loss_part[None]])
    grad_two = outer_cols(grad_pair, latent_pair)
    if whole:
        grad_two, grad_narrow, grad_dec_mid = together((grad_two, grad_narrow, grad_dec_mid))
        grad_dec_mid = rounded(halve(grad_dec_mid, 2, half))
        grad_narrow = halve(grad_narrow, 1)
    grad_a2, gain_two, shift_two = norm_back(grad_two, saved_two, norm_params, 1, cells)
    grad_enc_mid = inner_rows(one_low, grad_a2)
    grad_one = outer_cols(grad_a2, enc_mid_low)
    if whole:
        grad_one, grad_enc_mid, grad_narrow, grad_dec_mid = together(
            (grad_one, grad_enc_mid, grad_narrow, grad_dec_mid)
        )
        grad_dec_mid = unite(grad_dec_mid, 2)
        grad_enc_mid = halve(grad_enc_mid, 1, half)
        grad_narrow = halve(grad_narrow, 2)
    grad_a1, gain_one, shift_one = norm_back(grad_one, saved_one, norm_params, 0, cells)
    grad_enc_in = inner_rows(counts, grad_a1)
    if whole:
        encoder = scatter_pieces([grad_enc_in], [mom_enc_in])
        encoder, grad_enc_mid, grad_narrow, grad_dec_mid = together(
            (rounded(encoder), grad_enc_mid, grad_narrow, grad_dec_mid)
        )
        encoder, decoder = together((encoder, decoder))
        moment_first = cut_pieces(gather_block(encoder), [gene_local])[0]
        moment_out, moment_bias = cut_pieces(decoder, [gene_local, cell_count])
        grad_dec_mid = unite(grad_dec_mid, 1).astype(jnp.float32)
        grad_enc_mid = rounded(halve(grad_enc_mid, 2, half))
        grad_narrow = unite(grad_narrow, 2)
        grad_dec_mid, grad_enc_mid, grad_narrow = together(
            (grad_dec_mid, grad_enc_mid, grad_narrow)
        )
        grad_enc_mid = unite(unite(grad_enc_mid, 2), 1).astype(jnp.float32)
        grad_narrow = unite(grad_narrow, 1)
        own_moment_out = own_rows(moment_out)
    else:
        new_mom_enc_in = MOMENTUM * mom_enc_in + cell_sum(grad_enc_in)
        grad_enc_mid = cell_total(grad_enc_mid)
        grad_dec_mid = cell_total(grad_dec_mid)
        grad_narrow = cell_total(grad_narrow)
    small = cell_sum(small)
    grad_latent_bias = small[: 2 * latent_width].reshape(2, latent_width)
    total = small[2 * latent_width]
    moment_bias = moment_bias[:, : gene_local // cell_count].reshape(gene_count, gene_local)
    new_mom_out_bias = lax.dynamic_index_in_dim(moment_bias, gene_at, 0, keepdims=False)
    new_out_bias = vector_step(out_bias, new_mom_out_bias, jnp.mean(moment_bias * moment_bias))
    new_mom_dec_out = own_moment_out.T

    new_mom_enc_mid = MOMENTUM * mom_enc_mid + grad_enc_mid
    new_mom_dec_mid = MOMENTUM * mom_dec_mid + grad_dec_mid
    grad_latent = grad_narrow[: 2 * latent_width].reshape(2, latent_width, hidden_width)
    grad_dec_in = grad_narrow[2 * latent_width : 3 * latent_width]
    new_mom_dec_in = MOMENTUM * mom_dec_in + grad_dec_in
    turned_latent = MOMENTUM * jnp.swapaxes(mom_latent_w, 1, 2) + grad_latent
    new_mom_latent_w = jnp.swapaxes(turned_latent, 1, 2)
    narrow = orthogonal_narrow(jnp.concatenate([turned_latent, new_mom_dec_in[None]]))
    factor = math.sqrt(max(1.0, hidden_width / latent_width))
    new_dec_in = dec_in - RATE * factor * narrow[2]
    new_latent_w = latent_w - RATE * jnp.swapaxes(narrow[:2], 1, 2)
    if whole:
        square = orthogonal_squares(new_mom_enc_mid, new_mom_dec_mid)
        turned_enc_mid, turned_dec_mid = by_core(square)
        new_enc_mid = enc_mid - RATE * turned_enc_mid.astype(jnp.float32)
        new_dec_mid = dec_mid - RATE * turned_dec_mid.astype(jnp.float32)
        (
            moment_first,
            moment_out,
            new_mom_enc_mid,
            new_mom_dec_mid,
            new_mom_dec_out,
            new_mom_latent_w,
            new_dec_in,
            new_latent_w,
            new_enc_mid,
            new_dec_mid,
        ) = together(
            (
                moment_first,
                moment_out,
                new_mom_enc_mid,
                new_mom_dec_mid,
                new_mom_dec_out,
                new_mom_latent_w,
                new_dec_in,
                new_latent_w,
                new_enc_mid,
                new_dec_mid,
            )
        )
        new_mom_enc_in = own_rows(moment_first).astype(jnp.float32)
        turned_in, turned_out = by_core(orthogonal_talls(moment_first, moment_out, gene_local))
    else:
        turned_in = orthogonal_shared(new_mom_enc_in)
        turned_out = orthogonal_shared(own_moment_out)
        new_enc_mid = enc_mid - RATE * orthogonal_shared(new_mom_enc_mid, ())
        new_dec_mid = dec_mid - RATE * orthogonal_shared(new_mom_dec_mid, ())
    new_enc_in = enc_in - RATE * turned_in.astype(jnp.float32)
    factor = math.sqrt(max(1.0, genes / hidden_width))
    new_dec_out = dec_out - RATE * factor * turned_out.astype(jnp.float32).T

    grad_norm = jnp.stack(
        [
            jnp.stack([gain_one, gain_two, gain_three, gain_four]),
            jnp.stack([shift_one, shift_two, shift_three, shift_four]),
        ]
    )
    new_mom_norm = MOMENTUM * mom_norm + grad_norm
    new_norm = vector_step(
        norm_params, new_mom_norm, jnp.mean(new_mom_norm * new_mom_norm, axis=-1, keepdims=True)
    )
    new_mom_latent_bias = MOMENTUM * mom_latent_bias + grad_latent_bias
    new_latent_bias = vector_step(
        latent_bias,
        new_mom_latent_bias,
        jnp.mean(new_mom_latent_bias * new_mom_latent_bias, axis=-1, keepdims=True),
    )
    means = jnp.stack([saved_one[2], saved_two[2], saved_three[2], saved_four[2]])
    variances = jnp.stack([saved_one[3], saved_two[3], saved_three[3], saved_four[3]])
    new_running_mean = 0.9 * running_mean + 0.1 * means
    updated_running_variance = 0.9 * running_variance + 0.1 * variances * (cells / (cells - 1.0))
    return (
        recon,
        total / cells,
        new_enc_in,
        new_mom_enc_in,
        new_enc_mid,
        new_mom_enc_mid,
        new_latent_w,
        new_mom_latent_w,
        new_dec_in,
        new_mom_dec_in,
        new_dec_mid,
        new_mom_dec_mid,
        new_dec_out,
        new_mom_dec_out,
        new_norm,
        new_mom_norm,
        new_latent_bias,
        new_mom_latent_bias,
        new_out_bias,
        new_mom_out_bias,
        new_running_mean,
        updated_running_variance,
    )


def solution(mesh):
    in_specs = (
        P("cell", "gene"),
        P("cell"),
        P(None, "gene"),
        P(("cell", "gene"), None),
        P("gene", None),
        P(),
        P(),
        P(),
        P(),
        P(None, "gene"),
        P(),
        P(),
        P("gene"),
        P(),
        P(),
        P("gene", None),
        P(),
        P(),
        P(),
        P(),
        P(None, "gene"),
        P(),
        P(),
        P("gene"),
    )
    out_specs = (
        P("cell", "gene"),
        P(),
        P("gene", None),
        P("gene", None),
        P(),
        P(),
        P(),
        P(),
        P(),
        P(),
        P(),
        P(),
        P(None, "gene"),
        P(None, "gene"),
        P(),
        P(),
        P(),
        P(),
        P("gene"),
        P("gene"),
        P(),
        P(),
    )
    return jax.shard_map(shards, mesh=mesh, in_specs=in_specs, out_specs=out_specs, check_vma=False)
```

```python
import math

import jax
import jax.numpy as jnp
from jax import lax
from jax.experimental import pallas as pl
from jax.experimental.pallas import tpu as pltpu
from jax.sharding import PartitionSpec as P

NS = 5


EPSILON = 1e-05
ALPHA_KL = 5e-05
MOMENTUM = 0.95
RATE = 0.5
RATE_VECTOR = 0.2
COEF_A = 3.4445
COEF_B = -4.775
COEF_C = 2.0315


def inner_rows(left, right):
    return lax.dot_general(
        left, right, (((0,), (0,)), ((), ())), preferred_element_type=jnp.float32
    )


def outer_cols(left, right):
    return lax.dot_general(
        left, right, (((1,), (1,)), ((), ())), preferred_element_type=jnp.float32
    )


def rows_times(left, right):
    return jnp.dot(left, right, preferred_element_type=jnp.float32)


def low(values):
    return values.astype(jnp.bfloat16)


def pair_tree(values):
    while len(values) > 1:
        values = [values[at] + values[at + 1] for at in range(0, len(values), 2)]
    return values[0]


def swap(values, distance, axis):
    pairs = [(device, device ^ distance) for device in range(lax.axis_size(axis))]
    return lax.ppermute(values, axis, pairs)


def cell_sum(values):
    count = lax.axis_size("cell")
    if count & (count - 1):
        return lax.psum(values, "cell")
    return pair_tree(
        [values] + [swap(values, distance, "cell") for distance in range(1, count)]
    )


def cell_scatter(blocks):
    count = lax.axis_size("cell")
    me = lax.axis_index("cell")

    def block(owner):
        return lax.dynamic_index_in_dim(blocks, owner, 0, keepdims=False)

    return pair_tree(
        [block(me)]
        + [swap(block(me ^ distance), distance, "cell") for distance in range(1, count)]
    )


def first_gather(counts_turned, share):
    count = lax.axis_size("gene")
    me = lax.axis_index("gene")
    even = (me & 1) == 0
    ring = [(device, (device + 2) % count) for device in range(count)]
    steps = count // 2
    height, width = counts_turned.shape
    rows, depth = share.shape
    near = jnp.concatenate([counts_turned, lengthen(share, 1, width)])
    whole = jnp.zeros((count, height, width), counts_turned.dtype)
    shares = jnp.zeros((count, 4, rows, depth), share.dtype)
    at_x, at_core = {}, {}
    for step in range(steps + 2):
        moves = {}
        if step < steps:
            moves["far"] = swap(near, 1, "gene")
        if step < steps - 1:
            moves["near"] = lax.ppermute(near, "gene", ring)
        if step - 1 in at_x:
            moves["x"] = join(at_x[step - 1], 2, "cell", 1)
        if step - 2 in at_core:
            moves["core"] = join(at_core[step - 2], 1, "cell", 2)
        moves = lax.optimization_barrier(moves)
        if step < steps:
            source = (me + count - 2 * step) % count
            far = moves["far"]
            whole = lax.dynamic_update_index_in_dim(whole, near[:height], source, 0)
            whole = lax.dynamic_update_index_in_dim(whole, far[:height], source ^ 1, 0)
            own, other = near[height:, :depth], far[height:, :depth]
            at_x[step] = jnp.stack([jnp.where(even, own, other), jnp.where(even, other, own)])
        if step < steps - 1:
            near = moves["near"]
        if "x" in moves:
            at_core[step - 1] = moves["x"]
        if "core" in moves:
            base = (me + count - 2 * (step - 2)) % count - (me & 1)
            shares = lax.dynamic_update_slice(
                shares, moves["core"].reshape(2, 4, rows, depth), (base, 0, 0, 0)
            )
    return whole.reshape(count * height, width), shares.reshape(-1, depth)


def scatter_pieces(pieces, moments):
    count = lax.axis_size("cell")
    width = pieces[0].shape[1]

    def pack(entries):
        blocks = [entry.reshape(count, -1, width) for entry in entries]
        rows = sum(block.shape[1] for block in blocks)
        blocks.append(jnp.zeros((count, -rows % 8, width), jnp.float32))
        return jnp.concatenate(blocks, axis=1)

    known = [
        jnp.zeros_like(piece) if moment is None else MOMENTUM * moment
        for piece, moment in zip(pieces, moments)
    ]
    known = lax.dynamic_index_in_dim(pack(known), lax.axis_index("cell"), 0, keepdims=False)
    return cell_scatter(pack(pieces)) + known


def join(values, distance, axis, at):
    other = swap(values, distance, axis)
    upper = (lax.axis_index(axis) & distance) != 0
    return jnp.stack(
        [jnp.where(upper, other, values), jnp.where(upper, values, other)], axis=at
    )


def spread(values, axis, at=0):
    shape = values.shape
    distance = lax.axis_size(axis) // 2
    place = at
    while distance:
        values = join(values, distance, axis, place)
        distance //= 2
        place += 1
    return values.reshape(shape[:at] + (lax.axis_size(axis),) + shape[at:])


def cell_total(values):
    count = lax.axis_size("cell")
    distance = 1
    while distance < count:
        values = halve(values, distance)
        distance *= 2
    while distance > 1:
        distance //= 2
        values = unite(values, distance)
    return values


def by_core(mine):
    other = swap(mine, 1, "cell")
    odd = (lax.axis_index("cell") & 1) != 0
    return jnp.where(odd, other, mine), jnp.where(odd, mine, other)


def halve(values, distance, kind=jnp.float32):
    half = values.shape[0] // 2
    upper = ((lax.axis_index("cell") & distance) != 0).astype(jnp.int32)
    keep = lax.dynamic_slice_in_dim(values, upper * half, half, 0)
    give = lax.dynamic_slice_in_dim(values, (1 - upper) * half, half, 0)
    return keep + swap(give.astype(kind), distance, "cell").astype(jnp.float32)


def unite(values, distance):
    return join(values, distance, "cell", 0).reshape(-1, values.shape[1])


def rounded(values):
    return low(lax.reduce_precision(values, 8, 7))


def gather_block(block):
    return lax.all_gather(block, ("gene", "cell"), axis=0, tiled=False)


def cut_pieces(gathered, heights):
    count = lax.axis_size("cell")
    start = 0
    whole = []
    for height in heights:
        part = gathered[:, start : start + height // count]
        whole.append(part.reshape(-1, part.shape[2]))
        start += height // count
    return whole


def gather_slices(pieces, moments):
    slices = [
        cell_sum(piece) if moment is None else cell_sum(piece) + MOMENTUM * moment
        for piece, moment in zip(pieces, moments)
    ]
    return slices[:1] + [gather_rows(values, "gene") for values in slices[1:]]


def lengthen(values, axis, multiple):
    room = [(0, 0)] * values.ndim
    room[axis] = (0, -values.shape[axis] % multiple)
    return jnp.pad(values, room)


def three_parts(values):
    first = lax.reduce_precision(values, 8, 7)
    second = lax.reduce_precision(values - first, 8, 7)
    return low(jnp.stack([first, second, values - first - second], axis=1))


def gather_rows(values, axes):
    return lax.all_gather(values, axes, axis=0, tiled=True)


def rescale(values, batch_mean, inverse, norm_params, layer):
    scaled = (values - batch_mean) * inverse
    return scaled, scaled * norm_params[0, layer] + norm_params[1, layer]


def normalize(values, norm_params, layer, cells):
    totals = cell_sum(jnp.stack([jnp.sum(values, axis=0), jnp.sum(values * values, axis=0)]))
    batch_mean = totals[0] / cells
    batch_var = totals[1] / cells - batch_mean * batch_mean
    inverse = lax.rsqrt(batch_var + EPSILON)
    scaled, shifted = rescale(values, batch_mean, inverse, norm_params, layer)
    return (low(jax.nn.gelu(shifted)), (values, inverse, batch_mean, batch_var))


def norm_back(grad_out, saved, norm_params, layer, cells):
    values, inverse, batch_mean = lax.optimization_barrier(saved[:3])
    scaled, shifted = rescale(values, batch_mean, inverse, norm_params, layer)
    unused, pullback = jax.vjp(jax.nn.gelu, shifted)
    grad_shift = pullback(grad_out)[0]
    sums = cell_sum(jnp.stack([jnp.sum(grad_shift, axis=0), jnp.sum(grad_shift * scaled, axis=0)]))
    grad_in = (
        norm_params[0, layer] * inverse * (grad_shift - sums[0] / cells - scaled * sums[1] / cells)
    )
    return (low(grad_in), sums[1], sums[0])


def orthogonal_shared(own, axes="gene"):
    total = lax.psum(jnp.sum(own * own), axes)
    current = own / (jnp.sqrt(total) + 1e-07)
    for iteration in range(NS):
        operand = low(current)
        gram = lax.psum(inner_rows(operand, operand), axes)
        gram_low = low(gram)
        polynom = low(COEF_B * gram + COEF_C * rows_times(gram_low, gram_low))
        current = COEF_A * current + rows_times(operand, polynom)
    return current


def iterate(operand, gram, gram_low, polynom):
    width = gram.shape[0]
    spans = [(start, min(start + 256, width)) for start in range(0, width, 256)]

    def both_sides(target, start, stop, part):
        target[start:, start:stop] = low(part)
        if stop < width:
            target[start:stop, stop:] = low(part[stop - start :].T)

    for start, stop in spans:
        part = outer_cols(operand[start:, :], operand[start:stop, :])
        gram[start:, start:stop] = part
        both_sides(gram_low, start, stop, part)
    for start, stop in spans:
        square = outer_cols(gram_low[start:, :], gram_low[start:stop, :])
        part = COEF_B * gram[start:, start:stop] + COEF_C * square
        both_sides(polynom, start, stop, part)


def square_kernel(middle, square, current, operand, gram, gram_low, polynom):
    values = middle[...]
    current[...] = values * (1.0 / (jnp.sqrt(jnp.sum(values * values)) + 1e-07))

    def step(iteration, carry):
        operand[...] = low(current[...])
        iterate(operand, gram, gram_low, polynom)
        current[...] = COEF_A * current[...] + rows_times(polynom[...], operand[...])
        return carry

    lax.fori_loop(0, NS, step, 0)
    square[...] = low(current[...])


def tall_kernel(
    place, even, odd, tall, current, operand, own, own_low, gram, gram_low, polynom
):
    rows = even.shape[0]
    tile = 256

    def load(moment):
        def turn(at, total):
            here = pl.ds(pl.multiple_of(at * tile, tile), tile)
            values = moment[here, :].astype(jnp.float32)
            current[:, here] = values.T
            return total + jnp.sum(values * values)

        total = lax.fori_loop(0, rows // tile, turn, jnp.float32(0))
        scale = 1.0 / (jnp.sqrt(total) + 1e-07)

        def settle(at, carry):
            here = pl.ds(pl.multiple_of(at * tile, tile), tile)
            values = current[:, here] * scale
            current[:, here] = values
            operand[:, here] = low(values)
            return carry

        lax.fori_loop(0, rows // tile, settle, 0)
        mine = pl.ds(pl.multiple_of(place[1], 16), own.shape[1])
        own[...] = moment[mine, :].astype(jnp.float32).T * scale
        own_low[...] = low(own[...])

    pl.when(place[0] == 0)(lambda: load(even))
    pl.when(place[0] != 0)(lambda: load(odd))

    def step(iteration, carry):
        iterate(operand, gram, gram_low, polynom)
        own[...] = COEF_A * own[...] + rows_times(polynom[...], own_low[...])
        own_low[...] = low(own[...])

        @pl.when(iteration < NS - 1)
        def _():
            current[...] = COEF_A * current[...] + rows_times(polynom[...], operand[...])
            operand[...] = low(current[...])

        return carry

    lax.fori_loop(0, NS, step, 0)
    tall[...] = low(own[...].T)


def two_parts(values):
    first = low(values)
    return first, low(values - first.astype(jnp.float32))


def narrow_kernel(moments, results):
    count, rows = moments.shape[:2]

    def halves(values):
        return values[:rows] + values[rows:]

    def quarters(values):
        return halves(values[:, :rows] + values[:, rows:])

    for number in range(count):
        values = moments[number]
        results[number] = values * (1.0 / (jnp.sqrt(jnp.sum(values * values)) + 1e-07))

    def step(iteration, carry):
        for number in range(count):
            values = results[number]
            first, second = two_parts(values)
            stacked = jnp.concatenate([first, second], axis=0)
            gram = quarters(outer_cols(stacked, stacked))
            parts = two_parts(gram)
            square = quarters(
                rows_times(jnp.concatenate(parts, axis=0), jnp.concatenate(parts, axis=1))
            )
            parts = two_parts(COEF_B * gram + COEF_C * square)
            change = halves(rows_times(jnp.concatenate(parts, axis=0), first))
            results[number] = COEF_A * values + change + rows_times(parts[0], second)
        return carry

    lax.fori_loop(0, NS, step, 0)


def on_chip(kernel, shape, scratch, flops, *operands):
    space = pl.BlockSpec(memory_space=pltpu.VMEM)
    scalars = pl.BlockSpec(memory_space=pltpu.SMEM)
    return pl.pallas_call(
        kernel,
        out_shape=shape,
        in_specs=[scalars if operand.dtype == jnp.int32 else space for operand in operands],
        out_specs=jax.tree.map(lambda entry: space, shape),
        scratch_shapes=[pltpu.VMEM(*entry) for entry in scratch],
        compiler_params=pltpu.CompilerParams(vmem_limit_bytes=52 * 2**20),
        cost_estimate=pl.CostEstimate(flops=flops, bytes_accessed=2**22, transcendentals=0),
    )(*operands)


def orthogonal_squares(even, odd):
    width = even.shape[0]
    return on_chip(
        square_kernel,
        jax.ShapeDtypeStruct(even.shape, jnp.bfloat16),
        [
            ((width, width), jnp.float32),
            ((width, width), jnp.bfloat16),
            ((width, width), jnp.float32),
            ((width, width), jnp.bfloat16),
            ((width, width), jnp.bfloat16),
        ],
        width**2,
        jnp.where((lax.axis_index("cell") & 1) != 0, odd, even),
    )


def orthogonal_talls(even, odd, own_rows):
    rows, width = even.shape
    place = [lax.axis_index("cell") & 1, lax.axis_index("gene") * own_rows]
    return on_chip(
        tall_kernel,
        jax.ShapeDtypeStruct((own_rows, width), jnp.bfloat16),
        [
            ((width, rows), jnp.float32),
            ((width, rows), jnp.bfloat16),
            ((width, own_rows), jnp.float32),
            ((width, own_rows), jnp.bfloat16),
            ((width, width), jnp.float32),
            ((width, width), jnp.bfloat16),
            ((width, width), jnp.bfloat16),
        ],
        2 * NS * width * width * (2 * rows + width),
        jnp.stack(place).astype(jnp.int32),
        even,
        odd,
    )


def orthogonal_narrow(moments):
    count, width, length = moments.shape
    padded = lengthen(moments, 1, 128)
    return on_chip(
        narrow_kernel,
        jax.ShapeDtypeStruct(padded.shape, jnp.float32),
        [],
        8 * 10**9,
        padded,
    )[:, :width]


def vector_step(value, moment, square):
    return value - RATE_VECTOR * moment * lax.rsqrt(square + 1e-06)


def shards(
    counts,
    study,
    study_gene_mask,
    noise,
    enc_in,
    enc_mid,
    latent_w,
    dec_in,
    dec_mid,
    dec_out,
    norm_params,
    latent_bias,
    out_bias,
    running_mean,
    running_variance,
    mom_enc_in,
    mom_enc_mid,
    mom_latent_w,
    mom_dec_in,
    mom_dec_mid,
    mom_dec_out,
    mom_norm,
    mom_latent_bias,
    mom_out_bias,
):
    gene_count = lax.axis_size("gene")
    cell_count = lax.axis_size("cell")
    gene_at = lax.axis_index("gene")
    cell_at = lax.axis_index("cell")
    group_rows, gene_local = counts.shape
    cells = group_rows * cell_count
    genes = gene_local * gene_count
    hidden_width = enc_mid.shape[0]
    latent_width = dec_in.shape[0]
    study_labels = study_gene_mask.shape[0]
    devices = gene_count * cell_count
    whole = (
        group_rows * genes <= 2**22
        and genes * hidden_width <= 2**21
        and genes % 256 == 0
        and hidden_width % devices == 0
        and gene_local % (8 * cell_count) == 0
        and devices & (devices - 1) == 0
        and cell_count == 4
    )

    def own_rows(values, rows=gene_local):
        return lax.dynamic_slice_in_dim(values, gene_at * rows, rows, 0)

    selection = low(study[None, :] == jnp.arange(study_labels, dtype=jnp.int32)[:, None])
    enc_in_low = low(enc_in)
    enc_mid_low = low(enc_mid)
    latent_low = low(latent_w)
    dec_in_low = low(dec_in)
    dec_mid_low = low(dec_mid)
    dec_out_low = low(dec_out)
    counts_turned = counts.T
    last_layer = jnp.concatenate(
        [dec_out_low.T, low(study_gene_mask.T), three_parts(out_bias)], axis=1
    )
    if whole:
        part = gene_local // cell_count

        def own_part(values):
            return lax.dynamic_slice_in_dim(values, cell_at * part, part, 0)

        counts_turned, enc_in_low = first_gather(counts_turned, own_part(enc_in_low))
        last_layer = own_part(last_layer)
        counts_turned, last_layer, noise = lax.optimization_barrier(
            (counts_turned, last_layer, noise)
        )
        all_noise = spread(noise, "gene").reshape(group_rows, latent_width)
        first = inner_rows(counts_turned, enc_in_low)
        last_layer = gather_rows(last_layer, ("gene", "cell"))
    else:
        first = lax.psum(inner_rows(counts_turned, enc_in_low), "gene")
        all_noise = gather_rows(noise, "gene")
    dec_out_turned = last_layer[:, :hidden_width]
    mask_turned = last_layer[:, hidden_width : hidden_width + study_labels]
    bias_column = jnp.sum(
        last_layer[:, hidden_width + study_labels :].astype(jnp.float32), axis=1, keepdims=True
    )
    one_low, saved_one = normalize(first, norm_params, 0, cells)
    second = rows_times(one_low, enc_mid_low)
    two_low, saved_two = normalize(second, norm_params, 1, cells)
    latent_mean = rows_times(two_low, latent_low[0]) + latent_bias[0]
    latent_logvar = rows_times(two_low, latent_low[1]) + latent_bias[1]
    spread_factor = jnp.exp(0.5 * latent_logvar)
    sample_low = low(latent_mean + all_noise * spread_factor)
    third = rows_times(sample_low, dec_in_low)
    three_low, saved_three = normalize(third, norm_params, 2, cells)
    fourth = rows_times(three_low, dec_mid_low)
    four_low, saved_four = normalize(fourth, norm_params, 3, cells)
    decoded = outer_cols(dec_out_turned, four_low) + bias_column
    error = decoded - counts_turned.astype(jnp.float32)
    gene_mask = rows_times(mask_turned, selection)
    loss_part = 0.5 / genes * jnp.sum(gene_mask * error * error)
    grad_decoded = low(gene_mask * error / genes)
    grad_four = inner_rows(grad_decoded, dec_out_turned)
    if whole:
        own_grad = own_rows(grad_decoded)
    else:
        loss_part, grad_four = lax.psum((loss_part, grad_four), "gene")
        own_grad = grad_decoded
    recon = low(rows_times(four_low, dec_out_low) + out_bias)
    kl_scale = ALPHA_KL / genes
    loss_part = loss_part + kl_scale * 0.5 * jnp.sum(
        jnp.exp(latent_logvar) + latent_mean * latent_mean - 1.0 - latent_logvar
    )
    grad_dec_out = rows_times(own_grad, four_low)
    grad_out_bias = jnp.sum(own_grad, axis=1, dtype=jnp.float32)

    def bias_rows(values):
        return lengthen(values.reshape(cell_count, -1), 1, hidden_width)

    pieces = [grad_dec_out, bias_rows(grad_out_bias)]
    moments = [mom_dec_out.T, bias_rows(mom_out_bias)]
    if whole:
        decoder = scatter_pieces(pieces, moments)
    else:
        own_moment_out, moment_bias = gather_slices(pieces, moments)
    grad_a4, gain_four, shift_four = norm_back(grad_four, saved_four, norm_params, 3, cells)
    together = lax.optimization_barrier
    half = jnp.bfloat16
    grad_three = outer_cols(grad_a4, dec_mid_low)
    if whole:
        grad_three, decoder = together((grad_three, decoder))
        decoder = gather_block(decoder)
    grad_a3, gain_three, shift_three = norm_back(grad_three, saved_three, norm_params, 2, cells)
    grad_sample = outer_cols(grad_a3, dec_in_low)
    grad_mean = low(grad_sample + kl_scale * latent_mean)
    grad_logvar = low(
        grad_sample * all_noise * 0.5 * spread_factor
        + kl_scale * 0.5 * (jnp.exp(latent_logvar) - 1.0)
    )
    grad_pair = jnp.concatenate([grad_mean, grad_logvar], axis=1)
    latent_pair = jnp.concatenate([latent_low[0], latent_low[1]], axis=1)
    grad_two = outer_cols(grad_pair, latent_pair)
    grad_dec_mid = inner_rows(three_low, grad_a4)
    grad_narrow = jnp.concatenate([inner_rows(grad_pair, two_low), inner_rows(sample_low, grad_a3)])
    grad_narrow = lengthen(grad_narrow, 0, 8 * cell_count)
    if whole:
        grad_two, grad_dec_mid, grad_narrow = together((grad_two, grad_dec_mid, grad_narrow))
        grad_dec_mid = halve(grad_dec_mid, 1, half)
        grad_narrow = halve(grad_narrow, 1, half)
    grad_a2, gain_two, shift_two = norm_back(grad_two, saved_two, norm_params, 1, cells)
    grad_one = outer_cols(grad_a2, enc_mid_low)
    grad_a1, gain_one, shift_one = norm_back(grad_one, saved_one, norm_params, 0, cells)
    grad_enc_in = inner_rows(counts, grad_a1)
    grad_enc_in, grad_a2, grad_dec_mid, grad_narrow = together(
        (grad_enc_in, grad_a2, grad_dec_mid, grad_narrow)
    )
    if whole:
        encoder = rounded(scatter_pieces([grad_enc_in], [mom_enc_in]))
    grad_enc_mid = inner_rows(one_low, grad_a2)
    small = jnp.concatenate([jnp.sum(grad_pair, axis=0, dtype=jnp.float32), loss_part[None]])
    if whole:
        grad_dec_mid = rounded(halve(grad_dec_mid, 2, half))
        grad_enc_mid = halve(grad_enc_mid, 1, half)
        grad_narrow = rounded(halve(grad_narrow, 2, half))
        encoder, decoder = together((encoder, decoder))
        moment_first = cut_pieces(gather_block(encoder), [gene_local])[0]
        grad_dec_mid, grad_enc_mid, grad_narrow = together(
            (grad_dec_mid, grad_enc_mid, grad_narrow)
        )
        grad_dec_mid = unite(grad_dec_mid, 2)
        grad_enc_mid = rounded(halve(grad_enc_mid, 2, half))
        grad_narrow = unite(grad_narrow, 2)
        grad_dec_mid, grad_enc_mid, grad_narrow = together(
            (grad_dec_mid, grad_enc_mid, grad_narrow)
        )
        grad_dec_mid = unite(grad_dec_mid, 1).astype(jnp.float32)
        grad_enc_mid = unite(grad_enc_mid, 2)
        grad_narrow = unite(grad_narrow, 1).astype(jnp.float32)
        grad_dec_mid, grad_enc_mid, grad_narrow = together(
            (grad_dec_mid, grad_enc_mid, grad_narrow)
        )
        grad_enc_mid = unite(grad_enc_mid, 1)
        moment_out, moment_bias = cut_pieces(decoder, [gene_local, cell_count])
        own_moment_out = own_rows(moment_out)
    else:
        new_mom_enc_in = MOMENTUM * mom_enc_in + cell_sum(grad_enc_in)
        grad_enc_mid = cell_total(grad_enc_mid)
        grad_dec_mid = cell_total(grad_dec_mid)
        grad_narrow = cell_total(grad_narrow)
    grad_latent = grad_narrow[: 2 * latent_width].reshape(2, latent_width, hidden_width)
    grad_dec_in = grad_narrow[2 * latent_width : 3 * latent_width]
    new_mom_dec_in = MOMENTUM * mom_dec_in + grad_dec_in
    turned_latent = MOMENTUM * jnp.swapaxes(mom_latent_w, 1, 2) + grad_latent
    new_mom_latent_w = jnp.swapaxes(turned_latent, 1, 2)
    narrow = orthogonal_narrow(jnp.concatenate([turned_latent, new_mom_dec_in[None]]))
    small = cell_sum(small)
    grad_latent_bias = small[: 2 * latent_width].reshape(2, latent_width)
    total = small[2 * latent_width]
    moment_bias = moment_bias[:, : gene_local // cell_count].reshape(gene_count, gene_local)
    new_mom_out_bias = lax.dynamic_index_in_dim(moment_bias, gene_at, 0, keepdims=False)
    new_out_bias = vector_step(out_bias, new_mom_out_bias, jnp.mean(moment_bias * moment_bias))
    new_mom_dec_out = own_moment_out.T

    if whole:
        grad_enc_mid, narrow = together((grad_enc_mid, narrow))
        grad_enc_mid = grad_enc_mid.astype(jnp.float32)
    new_mom_enc_mid = MOMENTUM * mom_enc_mid + grad_enc_mid
    new_mom_dec_mid = MOMENTUM * mom_dec_mid + grad_dec_mid
    factor = math.sqrt(max(1.0, hidden_width / latent_width))
    new_dec_in = dec_in - RATE * factor * narrow[2]
    new_latent_w = latent_w - RATE * jnp.swapaxes(narrow[:2], 1, 2)
    if whole:
        square = orthogonal_squares(new_mom_enc_mid, new_mom_dec_mid)
        done = (new_mom_enc_mid, new_mom_dec_mid, new_mom_latent_w, new_dec_in, new_latent_w)
        turned, moment_first, moment_out, done = together(
            (by_core(square), moment_first, moment_out, done)
        )
        new_mom_enc_mid, new_mom_dec_mid, new_mom_latent_w, new_dec_in, new_latent_w = done
        turned_enc_mid, turned_dec_mid = turned
        new_enc_mid = enc_mid - RATE * turned_enc_mid.astype(jnp.float32)
        new_dec_mid = dec_mid - RATE * turned_dec_mid.astype(jnp.float32)
        new_mom_enc_in = own_rows(moment_first).astype(jnp.float32)
        turned_in, turned_out = by_core(orthogonal_talls(moment_first, moment_out, gene_local))
    else:
        turned_in = orthogonal_shared(new_mom_enc_in)
        turned_out = orthogonal_shared(own_moment_out)
        new_enc_mid = enc_mid - RATE * orthogonal_shared(new_mom_enc_mid, ())
        new_dec_mid = dec_mid - RATE * orthogonal_shared(new_mom_dec_mid, ())
    new_enc_in = enc_in - RATE * turned_in.astype(jnp.float32)
    factor = math.sqrt(max(1.0, genes / hidden_width))
    new_dec_out = dec_out - RATE * factor * turned_out.astype(jnp.float32).T

    grad_norm = jnp.stack(
        [
            jnp.stack([gain_one, gain_two, gain_three, gain_four]),
            jnp.stack([shift_one, shift_two, shift_three, shift_four]),
        ]
    )
    new_mom_norm = MOMENTUM * mom_norm + grad_norm
    new_norm = vector_step(
        norm_params, new_mom_norm, jnp.mean(new_mom_norm * new_mom_norm, axis=-1, keepdims=True)
    )
    new_mom_latent_bias = MOMENTUM * mom_latent_bias + grad_latent_bias
    new_latent_bias = vector_step(
        latent_bias,
        new_mom_latent_bias,
        jnp.mean(new_mom_latent_bias * new_mom_latent_bias, axis=-1, keepdims=True),
    )
    means = jnp.stack([saved_one[2], saved_two[2], saved_three[2], saved_four[2]])
    variances = jnp.stack([saved_one[3], saved_two[3], saved_three[3], saved_four[3]])
    new_running_mean = 0.9 * running_mean + 0.1 * means
    updated_running_variance = 0.9 * running_variance + 0.1 * variances * (cells / (cells - 1.0))
    return (
        recon,
        total / cells,
        new_enc_in,
        new_mom_enc_in,
        new_enc_mid,
        new_mom_enc_mid,
        new_latent_w,
        new_mom_latent_w,
        new_dec_in,
        new_mom_dec_in,
        new_dec_mid,
        new_mom_dec_mid,
        new_dec_out,
        new_mom_dec_out,
        new_norm,
        new_mom_norm,
        new_latent_bias,
        new_mom_latent_bias,
        new_out_bias,
        new_mom_out_bias,
        new_running_mean,
        updated_running_variance,
    )


def solution(mesh):
    in_specs = (
        P("cell", "gene"),
        P("cell"),
        P(None, "gene"),
        P(("cell", "gene"), None),
        P("gene", None),
        P(),
        P(),
        P(),
        P(),
        P(None, "gene"),
        P(),
        P(),
        P("gene"),
        P(),
        P(),
        P("gene", None),
        P(),
        P(),
        P(),
        P(),
        P(None, "gene"),
        P(),
        P(),
        P("gene"),
    )
    out_specs = (
        P("cell", "gene"),
        P(),
        P("gene", None),
        P("gene", None),
        P(),
        P(),
        P(),
        P(),
        P(),
        P(),
        P(),
        P(),
        P(None, "gene"),
        P(None, "gene"),
        P(),
        P(),
        P(),
        P(),
        P("gene"),
        P("gene"),
        P(),
        P(),
    )
    return jax.shard_map(shards, mesh=mesh, in_specs=in_specs, out_specs=out_specs, check_vma=False)
```

```python
import math

import jax
import jax.numpy as jnp
from jax import lax
from jax.experimental import pallas as pl
from jax.experimental.pallas import tpu as pltpu
from jax.sharding import PartitionSpec as P

NS = 5


EPSILON = 1e-05
ALPHA_KL = 5e-05
MOMENTUM = 0.95
RATE = 0.5
RATE_VECTOR = 0.2
COEF_A = 3.4445
COEF_B = -4.775
COEF_C = 2.0315


def inner_rows(left, right):
    return lax.dot_general(
        left, right, (((0,), (0,)), ((), ())), preferred_element_type=jnp.float32
    )


def outer_cols(left, right):
    return lax.dot_general(
        left, right, (((1,), (1,)), ((), ())), preferred_element_type=jnp.float32
    )


def rows_times(left, right):
    return jnp.dot(left, right, preferred_element_type=jnp.float32)


def low(values):
    return values.astype(jnp.bfloat16)


def pair_tree(values):
    while len(values) > 1:
        values = [values[at] + values[at + 1] for at in range(0, len(values), 2)]
    return values[0]


def swap(values, distance, axis):
    pairs = [(device, device ^ distance) for device in range(lax.axis_size(axis))]
    return lax.ppermute(values, axis, pairs)


def cell_sum(values):
    count = lax.axis_size("cell")
    if count & (count - 1):
        return lax.psum(values, "cell")
    return pair_tree(
        [values] + [swap(values, distance, "cell") for distance in range(1, count)]
    )


def cell_scatter(blocks):
    count = lax.axis_size("cell")
    me = lax.axis_index("cell")

    def block(owner):
        return lax.dynamic_index_in_dim(blocks, owner, 0, keepdims=False)

    return pair_tree(
        [block(me)]
        + [swap(block(me ^ distance), distance, "cell") for distance in range(1, count)]
    )


def first_gather(counts_turned, share):
    count = lax.axis_size("gene")
    me = lax.axis_index("gene")
    even = (me & 1) == 0
    ring = [(device, (device + 2) % count) for device in range(count)]
    steps = count // 2
    height, width = counts_turned.shape
    rows, depth = share.shape
    near = jnp.concatenate([counts_turned, lengthen(share, 1, width)])
    whole = jnp.zeros((count, height, width), counts_turned.dtype)
    shares = jnp.zeros((count, 4, rows, depth), share.dtype)
    at_x, at_core = {}, {}
    for step in range(steps + 2):
        moves = {}
        if step < steps:
            moves["far"] = swap(near, 1, "gene")
        if step < steps - 1:
            moves["near"] = lax.ppermute(near, "gene", ring)
        if step - 1 in at_x:
            moves["x"] = join(at_x[step - 1], 2, "cell", 1)
        if step - 2 in at_core:
            moves["core"] = join(at_core[step - 2], 1, "cell", 2)
        moves = lax.optimization_barrier(moves)
        if step < steps:
            source = (me + count - 2 * step) % count
            far = moves["far"]
            whole = lax.dynamic_update_index_in_dim(whole, near[:height], source, 0)
            whole = lax.dynamic_update_index_in_dim(whole, far[:height], source ^ 1, 0)
            own, other = near[height:, :depth], far[height:, :depth]
            at_x[step] = jnp.stack([jnp.where(even, own, other), jnp.where(even, other, own)])
        if step < steps - 1:
            near = moves["near"]
        if "x" in moves:
            at_core[step - 1] = moves["x"]
        if "core" in moves:
            base = (me + count - 2 * (step - 2)) % count - (me & 1)
            shares = lax.dynamic_update_slice(
                shares, moves["core"].reshape(2, 4, rows, depth), (base, 0, 0, 0)
            )
    return whole.reshape(count * height, width), shares.reshape(-1, depth)


def scatter_pieces(pieces, moments):
    count = lax.axis_size("cell")
    width = pieces[0].shape[1]

    def pack(entries):
        blocks = [entry.reshape(count, -1, width) for entry in entries]
        rows = sum(block.shape[1] for block in blocks)
        blocks.append(jnp.zeros((count, -rows % 8, width), jnp.float32))
        return jnp.concatenate(blocks, axis=1)

    known = [
        jnp.zeros_like(piece) if moment is None else MOMENTUM * moment
        for piece, moment in zip(pieces, moments)
    ]
    known = lax.dynamic_index_in_dim(pack(known), lax.axis_index("cell"), 0, keepdims=False)
    return cell_scatter(pack(pieces)) + known


def join(values, distance, axis, at):
    other = swap(values, distance, axis)
    upper = (lax.axis_index(axis) & distance) != 0
    return jnp.stack(
        [jnp.where(upper, other, values), jnp.where(upper, values, other)], axis=at
    )


def spread(values, axis, at=0):
    shape = values.shape
    distance = lax.axis_size(axis) // 2
    place = at
    while distance:
        values = join(values, distance, axis, place)
        distance //= 2
        place += 1
    return values.reshape(shape[:at] + (lax.axis_size(axis),) + shape[at:])


def cell_total(values):
    count = lax.axis_size("cell")
    distance = 1
    while distance < count:
        values = halve(values, distance)
        distance *= 2
    while distance > 1:
        distance //= 2
        values = unite(values, distance)
    return values


def by_core(mine):
    other = swap(mine, 1, "cell")
    odd = (lax.axis_index("cell") & 1) != 0
    return jnp.where(odd, other, mine), jnp.where(odd, mine, other)


def halve(values, distance, kind=jnp.float32):
    half = values.shape[0] // 2
    upper = ((lax.axis_index("cell") & distance) != 0).astype(jnp.int32)
    keep = lax.dynamic_slice_in_dim(values, upper * half, half, 0)
    give = lax.dynamic_slice_in_dim(values, (1 - upper) * half, half, 0)
    return keep + swap(give.astype(kind), distance, "cell").astype(jnp.float32)


def unite(values, distance):
    return join(values, distance, "cell", 0).reshape(-1, values.shape[1])


def rounded(values):
    return low(lax.reduce_precision(values, 8, 7))


def gather_block(block):
    return lax.all_gather(block, ("gene", "cell"), axis=0, tiled=False)


def cut_pieces(gathered, heights):
    count = lax.axis_size("cell")
    start = 0
    whole = []
    for height in heights:
        part = gathered[:, start : start + height // count]
        whole.append(part.reshape(-1, part.shape[2]))
        start += height // count
    return whole


def gather_slices(pieces, moments):
    slices = [
        cell_sum(piece) if moment is None else cell_sum(piece) + MOMENTUM * moment
        for piece, moment in zip(pieces, moments)
    ]
    return slices[:1] + [gather_rows(values, "gene") for values in slices[1:]]


def lengthen(values, axis, multiple):
    room = [(0, 0)] * values.ndim
    room[axis] = (0, -values.shape[axis] % multiple)
    return jnp.pad(values, room)


def three_parts(values):
    first = lax.reduce_precision(values, 8, 7)
    second = lax.reduce_precision(values - first, 8, 7)
    return low(jnp.stack([first, second, values - first - second], axis=1))


def gather_rows(values, axes):
    return lax.all_gather(values, axes, axis=0, tiled=True)


def rescale(values, batch_mean, inverse, norm_params, layer):
    scaled = (values - batch_mean) * inverse
    return scaled, scaled * norm_params[0, layer] + norm_params[1, layer]


def normalize(values, norm_params, layer, cells):
    totals = cell_sum(jnp.stack([jnp.sum(values, axis=0), jnp.sum(values * values, axis=0)]))
    batch_mean = totals[0] / cells
    batch_var = totals[1] / cells - batch_mean * batch_mean
    inverse = lax.rsqrt(batch_var + EPSILON)
    scaled, shifted = rescale(values, batch_mean, inverse, norm_params, layer)
    return (low(jax.nn.gelu(shifted)), (values, inverse, batch_mean, batch_var))


def norm_back(grad_out, saved, norm_params, layer, cells):
    values, inverse, batch_mean = lax.optimization_barrier(saved[:3])
    scaled, shifted = rescale(values, batch_mean, inverse, norm_params, layer)
    unused, pullback = jax.vjp(jax.nn.gelu, shifted)
    grad_shift = pullback(grad_out)[0]
    sums = cell_sum(jnp.stack([jnp.sum(grad_shift, axis=0), jnp.sum(grad_shift * scaled, axis=0)]))
    grad_in = (
        norm_params[0, layer] * inverse * (grad_shift - sums[0] / cells - scaled * sums[1] / cells)
    )
    return (low(grad_in), sums[1], sums[0])


def orthogonal_shared(own, axes="gene"):
    total = lax.psum(jnp.sum(own * own), axes)
    current = own / (jnp.sqrt(total) + 1e-07)
    for iteration in range(NS):
        operand = low(current)
        gram = lax.psum(inner_rows(operand, operand), axes)
        gram_low = low(gram)
        polynom = low(COEF_B * gram + COEF_C * rows_times(gram_low, gram_low))
        current = COEF_A * current + rows_times(operand, polynom)
    return current


def iterate(operand, gram, gram_low, polynom):
    width = gram.shape[0]
    spans = [(start, min(start + 256, width)) for start in range(0, width, 256)]

    def both_sides(target, start, stop, part):
        target[start:, start:stop] = low(part)
        if stop < width:
            target[start:stop, stop:] = low(part[stop - start :].T)

    for start, stop in spans:
        part = outer_cols(operand[start:, :], operand[start:stop, :])
        gram[start:, start:stop] = part
        both_sides(gram_low, start, stop, part)
    for start, stop in spans:
        square = outer_cols(gram_low[start:, :], gram_low[start:stop, :])
        part = COEF_B * gram[start:, start:stop] + COEF_C * square
        both_sides(polynom, start, stop, part)


def square_kernel(middle, square, current, operand, gram, gram_low, polynom):
    values = middle[...]
    current[...] = values * (1.0 / (jnp.sqrt(jnp.sum(values * values)) + 1e-07))

    def step(iteration, carry):
        operand[...] = low(current[...])
        iterate(operand, gram, gram_low, polynom)
        current[...] = COEF_A * current[...] + rows_times(polynom[...], operand[...])
        return carry

    lax.fori_loop(0, NS, step, 0)
    square[...] = low(current[...])


def tall_kernel(
    place, even, odd, tall, current, operand, own, own_low, gram, gram_low, polynom
):
    rows = even.shape[0]
    tile = 256

    def load(moment):
        def turn(at, total):
            here = pl.ds(pl.multiple_of(at * tile, tile), tile)
            values = moment[here, :].astype(jnp.float32)
            current[:, here] = values.T
            return total + jnp.sum(values * values)

        total = lax.fori_loop(0, rows // tile, turn, jnp.float32(0))
        scale = 1.0 / (jnp.sqrt(total) + 1e-07)

        def settle(at, carry):
            here = pl.ds(pl.multiple_of(at * tile, tile), tile)
            values = current[:, here] * scale
            current[:, here] = values
            operand[:, here] = low(values)
            return carry

        lax.fori_loop(0, rows // tile, settle, 0)
        mine = pl.ds(pl.multiple_of(place[1], 16), own.shape[1])
        own[...] = moment[mine, :].astype(jnp.float32).T * scale
        own_low[...] = low(own[...])

    pl.when(place[0] == 0)(lambda: load(even))
    pl.when(place[0] != 0)(lambda: load(odd))

    def step(iteration, carry):
        iterate(operand, gram, gram_low, polynom)
        own[...] = COEF_A * own[...] + rows_times(polynom[...], own_low[...])
        own_low[...] = low(own[...])

        @pl.when(iteration < NS - 1)
        def _():
            current[...] = COEF_A * current[...] + rows_times(polynom[...], operand[...])
            operand[...] = low(current[...])

        return carry

    lax.fori_loop(0, NS, step, 0)
    tall[...] = low(own[...].T)


def two_parts(values):
    first = low(values)
    return first, low(values - first.astype(jnp.float32))


def narrow_kernel(moments, results):
    count, rows = moments.shape[:2]

    def halves(values):
        return values[:rows] + values[rows:]

    def quarters(values):
        return halves(values[:, :rows] + values[:, rows:])

    for number in range(count):
        values = moments[number]
        results[number] = values * (1.0 / (jnp.sqrt(jnp.sum(values * values)) + 1e-07))

    def step(iteration, carry):
        for number in range(count):
            values = results[number]
            first, second = two_parts(values)
            stacked = jnp.concatenate([first, second], axis=0)
            gram = quarters(outer_cols(stacked, stacked))
            parts = two_parts(gram)
            square = quarters(
                rows_times(jnp.concatenate(parts, axis=0), jnp.concatenate(parts, axis=1))
            )
            parts = two_parts(COEF_B * gram + COEF_C * square)
            change = halves(rows_times(jnp.concatenate(parts, axis=0), first))
            results[number] = COEF_A * values + change + rows_times(parts[0], second)
        return carry

    lax.fori_loop(0, NS, step, 0)


def on_chip(kernel, shape, scratch, flops, *operands):
    space = pl.BlockSpec(memory_space=pltpu.VMEM)
    scalars = pl.BlockSpec(memory_space=pltpu.SMEM)
    return pl.pallas_call(
        kernel,
        out_shape=shape,
        in_specs=[scalars if operand.dtype == jnp.int32 else space for operand in operands],
        out_specs=jax.tree.map(lambda entry: space, shape),
        scratch_shapes=[pltpu.VMEM(*entry) for entry in scratch],
        compiler_params=pltpu.CompilerParams(vmem_limit_bytes=52 * 2**20),
        cost_estimate=pl.CostEstimate(flops=flops, bytes_accessed=2**22, transcendentals=0),
    )(*operands)


def orthogonal_squares(even, odd):
    width = even.shape[0]
    return on_chip(
        square_kernel,
        jax.ShapeDtypeStruct(even.shape, jnp.bfloat16),
        [
            ((width, width), jnp.float32),
            ((width, width), jnp.bfloat16),
            ((width, width), jnp.float32),
            ((width, width), jnp.bfloat16),
            ((width, width), jnp.bfloat16),
        ],
        width**2,
        jnp.where((lax.axis_index("cell") & 1) != 0, odd, even),
    )


def orthogonal_talls(even, odd, own_rows):
    rows, width = even.shape
    place = [lax.axis_index("cell") & 1, lax.axis_index("gene") * own_rows]
    return on_chip(
        tall_kernel,
        jax.ShapeDtypeStruct((own_rows, width), jnp.bfloat16),
        [
            ((width, rows), jnp.float32),
            ((width, rows), jnp.bfloat16),
            ((width, own_rows), jnp.float32),
            ((width, own_rows), jnp.bfloat16),
            ((width, width), jnp.float32),
            ((width, width), jnp.bfloat16),
            ((width, width), jnp.bfloat16),
        ],
        2 * NS * width * width * (2 * rows + width),
        jnp.stack(place).astype(jnp.int32),
        even,
        odd,
    )


def orthogonal_narrow(moments):
    count, width, length = moments.shape
    padded = lengthen(moments, 1, 128)
    return on_chip(
        narrow_kernel,
        jax.ShapeDtypeStruct(padded.shape, jnp.float32),
        [],
        8 * 10**9,
        padded,
    )[:, :width]


def vector_step(value, moment, square):
    return value - RATE_VECTOR * moment * lax.rsqrt(square + 1e-06)


def shards(
    counts,
    study,
    study_gene_mask,
    noise,
    enc_in,
    enc_mid,
    latent_w,
    dec_in,
    dec_mid,
    dec_out,
    norm_params,
    latent_bias,
    out_bias,
    running_mean,
    running_variance,
    mom_enc_in,
    mom_enc_mid,
    mom_latent_w,
    mom_dec_in,
    mom_dec_mid,
    mom_dec_out,
    mom_norm,
    mom_latent_bias,
    mom_out_bias,
):
    gene_count = lax.axis_size("gene")
    cell_count = lax.axis_size("cell")
    gene_at = lax.axis_index("gene")
    cell_at = lax.axis_index("cell")
    group_rows, gene_local = counts.shape
    cells = group_rows * cell_count
    genes = gene_local * gene_count
    hidden_width = enc_mid.shape[0]
    latent_width = dec_in.shape[0]
    study_labels = study_gene_mask.shape[0]
    devices = gene_count * cell_count
    whole = (
        group_rows * genes <= 2**22
        and genes * hidden_width <= 2**21
        and genes % 256 == 0
        and hidden_width % devices == 0
        and gene_local % (8 * cell_count) == 0
        and devices & (devices - 1) == 0
        and cell_count == 4
    )

    def own_rows(values, rows=gene_local):
        return lax.dynamic_slice_in_dim(values, gene_at * rows, rows, 0)

    selection = low(study[None, :] == jnp.arange(study_labels, dtype=jnp.int32)[:, None])
    enc_in_low = low(enc_in)
    enc_mid_low = low(enc_mid)
    latent_low = low(latent_w)
    dec_in_low = low(dec_in)
    dec_mid_low = low(dec_mid)
    dec_out_low = low(dec_out)
    counts_turned = counts.T
    last_layer = jnp.concatenate(
        [dec_out_low.T, low(study_gene_mask.T), three_parts(out_bias)], axis=1
    )
    if whole:
        part = gene_local // cell_count

        def own_part(values):
            return lax.dynamic_slice_in_dim(values, cell_at * part, part, 0)

        counts_turned, enc_in_low = first_gather(counts_turned, own_part(enc_in_low))
        last_layer = own_part(last_layer)
        counts_turned, last_layer, noise = lax.optimization_barrier(
            (counts_turned, last_layer, noise)
        )
        all_noise = spread(noise, "gene").reshape(group_rows, latent_width)
        first = inner_rows(counts_turned, enc_in_low)
        last_layer = gather_rows(last_layer, ("gene", "cell"))
    else:
        first = lax.psum(inner_rows(counts_turned, enc_in_low), "gene")
        all_noise = gather_rows(noise, "gene")
    dec_out_turned = last_layer[:, :hidden_width]
    mask_turned = last_layer[:, hidden_width : hidden_width + study_labels]
    bias_column = jnp.sum(
        last_layer[:, hidden_width + study_labels :].astype(jnp.float32), axis=1, keepdims=True
    )
    one_low, saved_one = normalize(first, norm_params, 0, cells)
    second = rows_times(one_low, enc_mid_low)
    two_low, saved_two = normalize(second, norm_params, 1, cells)
    latent_mean = rows_times(two_low, latent_low[0]) + latent_bias[0]
    latent_logvar = rows_times(two_low, latent_low[1]) + latent_bias[1]
    spread_factor = jnp.exp(0.5 * latent_logvar)
    sample_low = low(latent_mean + all_noise * spread_factor)
    third = rows_times(sample_low, dec_in_low)
    three_low, saved_three = normalize(third, norm_params, 2, cells)
    fourth = rows_times(three_low, dec_mid_low)
    four_low, saved_four = normalize(fourth, norm_params, 3, cells)
    decoded = outer_cols(dec_out_turned, four_low) + bias_column
    error = decoded - counts_turned.astype(jnp.float32)
    gene_mask = rows_times(mask_turned, selection)
    loss_part = 0.5 / genes * jnp.sum(gene_mask * error * error)
    grad_decoded = low(gene_mask * error / genes)
    grad_four = inner_rows(grad_decoded, dec_out_turned)
    if whole:
        own_grad = own_rows(grad_decoded)
    else:
        loss_part, grad_four = lax.psum((loss_part, grad_four), "gene")
        own_grad = grad_decoded
    recon = low(rows_times(four_low, dec_out_low) + out_bias)
    kl_scale = ALPHA_KL / genes
    loss_part = loss_part + kl_scale * 0.5 * jnp.sum(
        jnp.exp(latent_logvar) + latent_mean * latent_mean - 1.0 - latent_logvar
    )
    grad_dec_out = rows_times(own_grad, four_low)
    grad_out_bias = jnp.sum(own_grad, axis=1, dtype=jnp.float32)

    def bias_rows(values):
        return lengthen(values.reshape(cell_count, -1), 1, hidden_width)

    pieces = [grad_dec_out, bias_rows(grad_out_bias)]
    moments = [mom_dec_out.T, bias_rows(mom_out_bias)]
    if whole:
        decoder = scatter_pieces(pieces, moments)
    else:
        own_moment_out, moment_bias = gather_slices(pieces, moments)
    grad_a4, gain_four, shift_four = norm_back(grad_four, saved_four, norm_params, 3, cells)
    together = lax.optimization_barrier
    half = jnp.bfloat16
    grad_three = outer_cols(grad_a4, dec_mid_low)
    if whole:
        grad_three, decoder = together((grad_three, decoder))
        decoder = gather_block(decoder)
    grad_a3, gain_three, shift_three = norm_back(grad_three, saved_three, norm_params, 2, cells)
    grad_sample = outer_cols(grad_a3, dec_in_low)
    grad_mean = low(grad_sample + kl_scale * latent_mean)
    grad_logvar = low(
        grad_sample * all_noise * 0.5 * spread_factor
        + kl_scale * 0.5 * (jnp.exp(latent_logvar) - 1.0)
    )
    grad_pair = jnp.concatenate([grad_mean, grad_logvar], axis=1)
    latent_pair = jnp.concatenate([latent_low[0], latent_low[1]], axis=1)
    grad_two = outer_cols(grad_pair, latent_pair)
    grad_dec_mid = inner_rows(three_low, grad_a4)
    grad_narrow = jnp.concatenate([inner_rows(grad_pair, two_low), inner_rows(sample_low, grad_a3)])
    grad_narrow = lengthen(grad_narrow, 0, 8 * cell_count)
    if whole:
        grad_two, grad_dec_mid, grad_narrow = together((grad_two, grad_dec_mid, grad_narrow))
        grad_dec_mid = halve(grad_dec_mid, 1, half)
        grad_narrow = halve(grad_narrow, 1, half)
    grad_a2, gain_two, shift_two = norm_back(grad_two, saved_two, norm_params, 1, cells)
    grad_one = outer_cols(grad_a2, enc_mid_low)
    if whole:
        grad_one, grad_narrow = together((grad_one, grad_narrow))
        grad_narrow = rounded(halve(grad_narrow, 2, half))
    grad_a1, gain_one, shift_one = norm_back(grad_one, saved_one, norm_params, 0, cells)
    grad_enc_in = inner_rows(counts, grad_a1)
    def finish_narrow(grad_narrow):
        grad_latent = grad_narrow[: 2 * latent_width].reshape(2, latent_width, hidden_width)
        grad_dec_in = grad_narrow[2 * latent_width : 3 * latent_width]
        new_mom_dec_in = MOMENTUM * mom_dec_in + grad_dec_in
        turned_latent = MOMENTUM * jnp.swapaxes(mom_latent_w, 1, 2) + grad_latent
        new_mom_latent_w = jnp.swapaxes(turned_latent, 1, 2)
        narrow = orthogonal_narrow(jnp.concatenate([turned_latent, new_mom_dec_in[None]]))
        return new_mom_dec_in, new_mom_latent_w, narrow

    grad_enc_in, grad_a2, grad_dec_mid, grad_narrow = together(
        (grad_enc_in, grad_a2, grad_dec_mid, grad_narrow)
    )
    if whole:
        encoder = rounded(scatter_pieces([grad_enc_in], [mom_enc_in]))
    grad_enc_mid = inner_rows(one_low, grad_a2)
    small = jnp.concatenate([jnp.sum(grad_pair, axis=0, dtype=jnp.float32), loss_part[None]])
    if whole:
        grad_dec_mid = rounded(halve(grad_dec_mid, 2, half))
        grad_enc_mid = halve(grad_enc_mid, 1, half)
        grad_narrow = unite(grad_narrow, 2)
        encoder, decoder = together((encoder, decoder))
        moment_first = cut_pieces(gather_block(encoder), [gene_local])[0]
        grad_dec_mid, grad_enc_mid, grad_narrow = together(
            (grad_dec_mid, grad_enc_mid, grad_narrow)
        )
        grad_dec_mid = unite(grad_dec_mid, 2)
        grad_enc_mid = rounded(halve(grad_enc_mid, 2, half))
        grad_narrow = unite(grad_narrow, 1)
        grad_dec_mid, grad_enc_mid, grad_narrow = together(
            (grad_dec_mid, grad_enc_mid, grad_narrow)
        )
        grad_dec_mid = unite(grad_dec_mid, 1).astype(jnp.float32)
        grad_enc_mid = unite(grad_enc_mid, 2)
        finished = finish_narrow(grad_narrow.astype(jnp.float32))
        grad_dec_mid, grad_enc_mid, finished = together((grad_dec_mid, grad_enc_mid, finished))
        new_mom_dec_in, new_mom_latent_w, narrow = finished
        grad_enc_mid = unite(grad_enc_mid, 1)
        moment_out, moment_bias = cut_pieces(decoder, [gene_local, cell_count])
        own_moment_out = own_rows(moment_out)
    else:
        new_mom_enc_in = MOMENTUM * mom_enc_in + cell_sum(grad_enc_in)
        grad_enc_mid = cell_total(grad_enc_mid)
        grad_dec_mid = cell_total(grad_dec_mid)
        grad_narrow = cell_total(grad_narrow)
    if not whole:
        new_mom_dec_in, new_mom_latent_w, narrow = finish_narrow(grad_narrow)
    small = cell_sum(small)
    grad_latent_bias = small[: 2 * latent_width].reshape(2, latent_width)
    total = small[2 * latent_width]
    moment_bias = moment_bias[:, : gene_local // cell_count].reshape(gene_count, gene_local)
    new_mom_out_bias = lax.dynamic_index_in_dim(moment_bias, gene_at, 0, keepdims=False)
    new_out_bias = vector_step(out_bias, new_mom_out_bias, jnp.mean(moment_bias * moment_bias))
    new_mom_dec_out = own_moment_out.T

    if whole:
        grad_enc_mid = grad_enc_mid.astype(jnp.float32)
    new_mom_enc_mid = MOMENTUM * mom_enc_mid + grad_enc_mid
    new_mom_dec_mid = MOMENTUM * mom_dec_mid + grad_dec_mid
    factor = math.sqrt(max(1.0, hidden_width / latent_width))
    new_dec_in = dec_in - RATE * factor * narrow[2]
    new_latent_w = latent_w - RATE * jnp.swapaxes(narrow[:2], 1, 2)
    if whole:
        square = orthogonal_squares(new_mom_enc_mid, new_mom_dec_mid)
        done = (new_mom_enc_mid, new_mom_dec_mid, new_mom_latent_w, new_dec_in, new_latent_w)
        turned, moment_first, moment_out, done = together(
            (by_core(square), moment_first, moment_out, done)
        )
        new_mom_enc_mid, new_mom_dec_mid, new_mom_latent_w, new_dec_in, new_latent_w = done
        turned_enc_mid, turned_dec_mid = turned
        new_enc_mid = enc_mid - RATE * turned_enc_mid.astype(jnp.float32)
        new_dec_mid = dec_mid - RATE * turned_dec_mid.astype(jnp.float32)
        new_mom_enc_in = own_rows(moment_first).astype(jnp.float32)
        turned_in, turned_out = by_core(orthogonal_talls(moment_first, moment_out, gene_local))
    else:
        turned_in = orthogonal_shared(new_mom_enc_in)
        turned_out = orthogonal_shared(own_moment_out)
        new_enc_mid = enc_mid - RATE * orthogonal_shared(new_mom_enc_mid, ())
        new_dec_mid = dec_mid - RATE * orthogonal_shared(new_mom_dec_mid, ())
    new_enc_in = enc_in - RATE * turned_in.astype(jnp.float32)
    factor = math.sqrt(max(1.0, genes / hidden_width))
    new_dec_out = dec_out - RATE * factor * turned_out.astype(jnp.float32).T

    grad_norm = jnp.stack(
        [
            jnp.stack([gain_one, gain_two, gain_three, gain_four]),
            jnp.stack([shift_one, shift_two, shift_three, shift_four]),
        ]
    )
    new_mom_norm = MOMENTUM * mom_norm + grad_norm
    new_norm = vector_step(
        norm_params, new_mom_norm, jnp.mean(new_mom_norm * new_mom_norm, axis=-1, keepdims=True)
    )
    new_mom_latent_bias = MOMENTUM * mom_latent_bias + grad_latent_bias
    new_latent_bias = vector_step(
        latent_bias,
        new_mom_latent_bias,
        jnp.mean(new_mom_latent_bias * new_mom_latent_bias, axis=-1, keepdims=True),
    )
    means = jnp.stack([saved_one[2], saved_two[2], saved_three[2], saved_four[2]])
    variances = jnp.stack([saved_one[3], saved_two[3], saved_three[3], saved_four[3]])
    new_running_mean = 0.9 * running_mean + 0.1 * means
    updated_running_variance = 0.9 * running_variance + 0.1 * variances * (cells / (cells - 1.0))
    return (
        recon,
        total / cells,
        new_enc_in,
        new_mom_enc_in,
        new_enc_mid,
        new_mom_enc_mid,
        new_latent_w,
        new_mom_latent_w,
        new_dec_in,
        new_mom_dec_in,
        new_dec_mid,
        new_mom_dec_mid,
        new_dec_out,
        new_mom_dec_out,
        new_norm,
        new_mom_norm,
        new_latent_bias,
        new_mom_latent_bias,
        new_out_bias,
        new_mom_out_bias,
        new_running_mean,
        updated_running_variance,
    )


def solution(mesh):
    in_specs = (
        P("cell", "gene"),
        P("cell"),
        P(None, "gene"),
        P(("cell", "gene"), None),
        P("gene", None),
        P(),
        P(),
        P(),
        P(),
        P(None, "gene"),
        P(),
        P(),
        P("gene"),
        P(),
        P(),
        P("gene", None),
        P(),
        P(),
        P(),
        P(),
        P(None, "gene"),
        P(),
        P(),
        P("gene"),
    )
    out_specs = (
        P("cell", "gene"),
        P(),
        P("gene", None),
        P("gene", None),
        P(),
        P(),
        P(),
        P(),
        P(),
        P(),
        P(),
        P(),
        P(None, "gene"),
        P(None, "gene"),
        P(),
        P(),
        P(),
        P(),
        P("gene"),
        P("gene"),
        P(),
        P(),
    )
    return jax.shard_map(shards, mesh=mesh, in_specs=in_specs, out_specs=out_specs, check_vma=False)
```

```python
import math

import jax
import jax.numpy as jnp
from jax import lax
from jax.experimental import pallas as pl
from jax.experimental.pallas import tpu as pltpu
from jax.sharding import PartitionSpec as P

NS = 5


EPSILON = 1e-05
ALPHA_KL = 5e-05
MOMENTUM = 0.95
RATE = 0.5
RATE_VECTOR = 0.2
COEF_A = 3.4445
COEF_B = -4.775
COEF_C = 2.0315


def inner_rows(left, right):
    return lax.dot_general(
        left, right, (((0,), (0,)), ((), ())), preferred_element_type=jnp.float32
    )


def outer_cols(left, right):
    return lax.dot_general(
        left, right, (((1,), (1,)), ((), ())), preferred_element_type=jnp.float32
    )


def rows_times(left, right):
    return jnp.dot(left, right, preferred_element_type=jnp.float32)


def low(values):
    return values.astype(jnp.bfloat16)


def pair_tree(values):
    while len(values) > 1:
        values = [values[at] + values[at + 1] for at in range(0, len(values), 2)]
    return values[0]


def swap(values, distance, axis):
    pairs = [(device, device ^ distance) for device in range(lax.axis_size(axis))]
    return lax.ppermute(values, axis, pairs)


def cell_sum(values):
    count = lax.axis_size("cell")
    if count & (count - 1):
        return lax.psum(values, "cell")
    return pair_tree(
        [values] + [swap(values, distance, "cell") for distance in range(1, count)]
    )


def cell_scatter(blocks, kind=jnp.float32):
    count = lax.axis_size("cell")
    me = lax.axis_index("cell")

    def block(owner):
        return lax.dynamic_index_in_dim(blocks, owner, 0, keepdims=False)

    return pair_tree(
        [block(me)]
        + [
            swap(block(me ^ distance).astype(kind), distance, "cell").astype(jnp.float32)
            for distance in range(1, count)
        ]
    )


def first_gather(counts_turned, share):
    count = lax.axis_size("gene")
    me = lax.axis_index("gene")
    even = (me & 1) == 0
    ring = [(device, (device + 2) % count) for device in range(count)]
    steps = count // 2
    height, width = counts_turned.shape
    rows, depth = share.shape
    near = jnp.concatenate([counts_turned, lengthen(share, 1, width)])
    whole = jnp.zeros((count, height, width), counts_turned.dtype)
    shares = jnp.zeros((count, 4, rows, depth), share.dtype)
    at_x, at_core = {}, {}
    for step in range(steps + 2):
        moves = {}
        if step < steps:
            moves["far"] = swap(near, 1, "gene")
        if step < steps - 1:
            moves["near"] = lax.ppermute(near, "gene", ring)
        if step - 1 in at_x:
            moves["x"] = join(at_x[step - 1], 2, "cell", 1)
        if step - 2 in at_core:
            moves["core"] = join(at_core[step - 2], 1, "cell", 2)
        moves = lax.optimization_barrier(moves)
        if step < steps:
            source = (me + count - 2 * step) % count
            far = moves["far"]
            whole = lax.dynamic_update_index_in_dim(whole, near[:height], source, 0)
            whole = lax.dynamic_update_index_in_dim(whole, far[:height], source ^ 1, 0)
            own, other = near[height:, :depth], far[height:, :depth]
            at_x[step] = jnp.stack([jnp.where(even, own, other), jnp.where(even, other, own)])
        if step < steps - 1:
            near = moves["near"]
        if "x" in moves:
            at_core[step - 1] = moves["x"]
        if "core" in moves:
            base = (me + count - 2 * (step - 2)) % count - (me & 1)
            shares = lax.dynamic_update_slice(
                shares, moves["core"].reshape(2, 4, rows, depth), (base, 0, 0, 0)
            )
    return whole.reshape(count * height, width), shares.reshape(-1, depth)


def scatter_pieces(pieces, moments, kind=jnp.float32):
    count = lax.axis_size("cell")
    width = pieces[0].shape[1]

    def pack(entries):
        blocks = [entry.reshape(count, -1, width) for entry in entries]
        rows = sum(block.shape[1] for block in blocks)
        blocks.append(jnp.zeros((count, -rows % 8, width), jnp.float32))
        return jnp.concatenate(blocks, axis=1)

    known = [
        jnp.zeros_like(piece) if moment is None else MOMENTUM * moment
        for piece, moment in zip(pieces, moments)
    ]
    known = lax.dynamic_index_in_dim(pack(known), lax.axis_index("cell"), 0, keepdims=False)
    return cell_scatter(pack(pieces), kind) + known


def join(values, distance, axis, at):
    other = swap(values, distance, axis)
    upper = (lax.axis_index(axis) & distance) != 0
    return jnp.stack(
        [jnp.where(upper, other, values), jnp.where(upper, values, other)], axis=at
    )


def spread(values, axis, at=0):
    shape = values.shape
    distance = lax.axis_size(axis) // 2
    place = at
    while distance:
        values = join(values, distance, axis, place)
        distance //= 2
        place += 1
    return values.reshape(shape[:at] + (lax.axis_size(axis),) + shape[at:])


def cell_total(values):
    count = lax.axis_size("cell")
    distance = 1
    while distance < count:
        values = halve(values, distance)
        distance *= 2
    while distance > 1:
        distance //= 2
        values = unite(values, distance)
    return values


def by_core(mine):
    other = swap(mine, 1, "cell")
    odd = (lax.axis_index("cell") & 1) != 0
    return jnp.where(odd, other, mine), jnp.where(odd, mine, other)


def halve(values, distance, kind=jnp.float32):
    half = values.shape[0] // 2
    upper = ((lax.axis_index("cell") & distance) != 0).astype(jnp.int32)
    keep = lax.dynamic_slice_in_dim(values, upper * half, half, 0)
    give = lax.dynamic_slice_in_dim(values, (1 - upper) * half, half, 0)
    return keep + swap(give.astype(kind), distance, "cell").astype(jnp.float32)


def unite(values, distance):
    return join(values, distance, "cell", 0).reshape(-1, values.shape[1])


def rounded(values):
    return low(lax.reduce_precision(values, 8, 7))


def gather_block(block):
    return lax.all_gather(block, ("gene", "cell"), axis=0, tiled=False)


def cut_pieces(gathered, heights):
    count = lax.axis_size("cell")
    start = 0
    whole = []
    for height in heights:
        part = gathered[:, start : start + height // count]
        whole.append(part.reshape(-1, part.shape[2]))
        start += height // count
    return whole


def gather_slices(pieces, moments):
    slices = [
        cell_sum(piece) if moment is None else cell_sum(piece) + MOMENTUM * moment
        for piece, moment in zip(pieces, moments)
    ]
    return slices[:1] + [gather_rows(values, "gene") for values in slices[1:]]


def lengthen(values, axis, multiple):
    room = [(0, 0)] * values.ndim
    room[axis] = (0, -values.shape[axis] % multiple)
    return jnp.pad(values, room)


def three_parts(values):
    first = lax.reduce_precision(values, 8, 7)
    second = lax.reduce_precision(values - first, 8, 7)
    return low(jnp.stack([first, second, values - first - second], axis=1))


def gather_rows(values, axes):
    return lax.all_gather(values, axes, axis=0, tiled=True)


def rescale(values, batch_mean, inverse, norm_params, layer):
    scaled = (values - batch_mean) * inverse
    return scaled, scaled * norm_params[0, layer] + norm_params[1, layer]


def normalize(values, norm_params, layer, cells):
    totals = cell_sum(jnp.stack([jnp.sum(values, axis=0), jnp.sum(values * values, axis=0)]))
    batch_mean = totals[0] / cells
    batch_var = totals[1] / cells - batch_mean * batch_mean
    inverse = lax.rsqrt(batch_var + EPSILON)
    scaled, shifted = rescale(values, batch_mean, inverse, norm_params, layer)
    return (low(jax.nn.gelu(shifted)), (values, inverse, batch_mean, batch_var))


def norm_back(grad_out, saved, norm_params, layer, cells):
    values, inverse, batch_mean = lax.optimization_barrier(saved[:3])
    scaled, shifted = rescale(values, batch_mean, inverse, norm_params, layer)
    unused, pullback = jax.vjp(jax.nn.gelu, shifted)
    grad_shift = pullback(grad_out)[0]
    sums = cell_sum(jnp.stack([jnp.sum(grad_shift, axis=0), jnp.sum(grad_shift * scaled, axis=0)]))
    grad_in = (
        norm_params[0, layer] * inverse * (grad_shift - sums[0] / cells - scaled * sums[1] / cells)
    )
    return (low(grad_in), sums[1], sums[0])


def orthogonal_shared(own, axes="gene"):
    total = lax.psum(jnp.sum(own * own), axes)
    current = own / (jnp.sqrt(total) + 1e-07)
    for iteration in range(NS):
        operand = low(current)
        gram = lax.psum(inner_rows(operand, operand), axes)
        gram_low = low(gram)
        polynom = low(COEF_B * gram + COEF_C * rows_times(gram_low, gram_low))
        current = COEF_A * current + rows_times(operand, polynom)
    return current


def iterate(operand, gram, gram_low, polynom):
    width = gram.shape[0]
    spans = [(start, min(start + 256, width)) for start in range(0, width, 256)]

    def both_sides(target, start, stop, part):
        target[start:, start:stop] = low(part)
        if stop < width:
            target[start:stop, stop:] = low(part[stop - start :].T)

    for start, stop in spans:
        part = outer_cols(operand[start:, :], operand[start:stop, :])
        gram[start:, start:stop] = part
        both_sides(gram_low, start, stop, part)
    for start, stop in spans:
        square = outer_cols(gram_low[start:, :], gram_low[start:stop, :])
        part = COEF_B * gram[start:, start:stop] + COEF_C * square
        both_sides(polynom, start, stop, part)


def square_kernel(middle, square, current, operand, gram, gram_low, polynom):
    values = middle[...]
    current[...] = values * (1.0 / (jnp.sqrt(jnp.sum(values * values)) + 1e-07))

    def step(iteration, carry):
        operand[...] = low(current[...])
        iterate(operand, gram, gram_low, polynom)
        current[...] = COEF_A * current[...] + rows_times(polynom[...], operand[...])
        return carry

    lax.fori_loop(0, NS, step, 0)
    square[...] = low(current[...])


def tall_kernel(
    place, even, odd, tall, current, operand, own, own_low, gram, gram_low, polynom
):
    rows = even.shape[0]
    tile = 256

    def load(moment):
        def turn(at, total):
            here = pl.ds(pl.multiple_of(at * tile, tile), tile)
            values = moment[here, :].astype(jnp.float32)
            current[:, here] = values.T
            return total + jnp.sum(values * values)

        total = lax.fori_loop(0, rows // tile, turn, jnp.float32(0))
        scale = 1.0 / (jnp.sqrt(total) + 1e-07)

        def settle(at, carry):
            here = pl.ds(pl.multiple_of(at * tile, tile), tile)
            values = current[:, here] * scale
            current[:, here] = values
            operand[:, here] = low(values)
            return carry

        lax.fori_loop(0, rows // tile, settle, 0)
        mine = pl.ds(pl.multiple_of(place[1], 16), own.shape[1])
        own[...] = moment[mine, :].astype(jnp.float32).T * scale
        own_low[...] = low(own[...])

    pl.when(place[0] == 0)(lambda: load(even))
    pl.when(place[0] != 0)(lambda: load(odd))

    def step(iteration, carry):
        iterate(operand, gram, gram_low, polynom)
        own[...] = COEF_A * own[...] + rows_times(polynom[...], own_low[...])
        own_low[...] = low(own[...])

        @pl.when(iteration < NS - 1)
        def _():
            current[...] = COEF_A * current[...] + rows_times(polynom[...], operand[...])
            operand[...] = low(current[...])

        return carry

    lax.fori_loop(0, NS, step, 0)
    tall[...] = low(own[...].T)


def two_parts(values):
    first = low(values)
    return first, low(values - first.astype(jnp.float32))


def narrow_kernel(moments, results):
    count, rows = moments.shape[:2]

    def halves(values):
        return values[:rows] + values[rows:]

    def quarters(values):
        return halves(values[:, :rows] + values[:, rows:])

    for number in range(count):
        values = moments[number]
        results[number] = values * (1.0 / (jnp.sqrt(jnp.sum(values * values)) + 1e-07))

    def step(iteration, carry):
        for number in range(count):
            values = results[number]
            first, second = two_parts(values)
            stacked = jnp.concatenate([first, second], axis=0)
            gram = quarters(outer_cols(stacked, stacked))
            parts = two_parts(gram)
            square = quarters(
                rows_times(jnp.concatenate(parts, axis=0), jnp.concatenate(parts, axis=1))
            )
            parts = two_parts(COEF_B * gram + COEF_C * square)
            change = halves(rows_times(jnp.concatenate(parts, axis=0), first))
            results[number] = COEF_A * values + change + rows_times(parts[0], second)
        return carry

    lax.fori_loop(0, NS, step, 0)


def on_chip(kernel, shape, scratch, flops, *operands):
    space = pl.BlockSpec(memory_space=pltpu.VMEM)
    scalars = pl.BlockSpec(memory_space=pltpu.SMEM)
    return pl.pallas_call(
        kernel,
        out_shape=shape,
        in_specs=[scalars if operand.dtype == jnp.int32 else space for operand in operands],
        out_specs=jax.tree.map(lambda entry: space, shape),
        scratch_shapes=[pltpu.VMEM(*entry) for entry in scratch],
        compiler_params=pltpu.CompilerParams(vmem_limit_bytes=52 * 2**20),
        cost_estimate=pl.CostEstimate(flops=flops, bytes_accessed=2**22, transcendentals=0),
    )(*operands)


def orthogonal_squares(even, odd):
    width = even.shape[0]
    return on_chip(
        square_kernel,
        jax.ShapeDtypeStruct(even.shape, jnp.bfloat16),
        [
            ((width, width), jnp.float32),
            ((width, width), jnp.bfloat16),
            ((width, width), jnp.float32),
            ((width, width), jnp.bfloat16),
            ((width, width), jnp.bfloat16),
        ],
        width**2,
        jnp.where((lax.axis_index("cell") & 1) != 0, odd, even),
    )


def orthogonal_talls(even, odd, own_rows):
    rows, width = even.shape
    place = [lax.axis_index("cell") & 1, lax.axis_index("gene") * own_rows]
    return on_chip(
        tall_kernel,
        jax.ShapeDtypeStruct((own_rows, width), jnp.bfloat16),
        [
            ((width, rows), jnp.float32),
            ((width, rows), jnp.bfloat16),
            ((width, own_rows), jnp.float32),
            ((width, own_rows), jnp.bfloat16),
            ((width, width), jnp.float32),
            ((width, width), jnp.bfloat16),
            ((width, width), jnp.bfloat16),
        ],
        2 * NS * width * width * (2 * rows + width),
        jnp.stack(place).astype(jnp.int32),
        even,
        odd,
    )


def orthogonal_narrow(moments):
    count, width, length = moments.shape
    padded = lengthen(moments, 1, 128)
    return on_chip(
        narrow_kernel,
        jax.ShapeDtypeStruct(padded.shape, jnp.float32),
        [],
        8 * 10**9,
        padded,
    )[:, :width]


def vector_step(value, moment, square):
    return value - RATE_VECTOR * moment * lax.rsqrt(square + 1e-06)


def shards(
    counts,
    study,
    study_gene_mask,
    noise,
    enc_in,
    enc_mid,
    latent_w,
    dec_in,
    dec_mid,
    dec_out,
    norm_params,
    latent_bias,
    out_bias,
    running_mean,
    running_variance,
    mom_enc_in,
    mom_enc_mid,
    mom_latent_w,
    mom_dec_in,
    mom_dec_mid,
    mom_dec_out,
    mom_norm,
    mom_latent_bias,
    mom_out_bias,
):
    gene_count = lax.axis_size("gene")
    cell_count = lax.axis_size("cell")
    gene_at = lax.axis_index("gene")
    cell_at = lax.axis_index("cell")
    group_rows, gene_local = counts.shape
    cells = group_rows * cell_count
    genes = gene_local * gene_count
    hidden_width = enc_mid.shape[0]
    latent_width = dec_in.shape[0]
    study_labels = study_gene_mask.shape[0]
    devices = gene_count * cell_count
    whole = (
        group_rows * genes <= 2**22
        and genes * hidden_width <= 2**21
        and genes % 256 == 0
        and hidden_width % devices == 0
        and gene_local % (8 * cell_count) == 0
        and devices & (devices - 1) == 0
        and cell_count == 4
    )

    def own_rows(values, rows=gene_local):
        return lax.dynamic_slice_in_dim(values, gene_at * rows, rows, 0)

    selection = low(study[None, :] == jnp.arange(study_labels, dtype=jnp.int32)[:, None])
    enc_in_low = low(enc_in)
    enc_mid_low = low(enc_mid)
    latent_low = low(latent_w)
    dec_in_low = low(dec_in)
    dec_mid_low = low(dec_mid)
    dec_out_low = low(dec_out)
    counts_turned = counts.T
    last_layer = jnp.concatenate(
        [dec_out_low.T, low(study_gene_mask.T), three_parts(out_bias)], axis=1
    )
    if whole:
        part = gene_local // cell_count

        def own_part(values):
            return lax.dynamic_slice_in_dim(values, cell_at * part, part, 0)

        counts_turned, enc_in_low = first_gather(counts_turned, own_part(enc_in_low))
        last_layer = own_part(last_layer)
        counts_turned, last_layer, noise = lax.optimization_barrier(
            (counts_turned, last_layer, noise)
        )
        all_noise = spread(noise, "gene").reshape(group_rows, latent_width)
        first = inner_rows(counts_turned, enc_in_low)
        last_layer = gather_rows(last_layer, ("gene", "cell"))
    else:
        first = lax.psum(inner_rows(counts_turned, enc_in_low), "gene")
        all_noise = gather_rows(noise, "gene")
    dec_out_turned = last_layer[:, :hidden_width]
    mask_turned = last_layer[:, hidden_width : hidden_width + study_labels]
    bias_column = jnp.sum(
        last_layer[:, hidden_width + study_labels :].astype(jnp.float32), axis=1, keepdims=True
    )
    one_low, saved_one = normalize(first, norm_params, 0, cells)
    second = rows_times(one_low, enc_mid_low)
    two_low, saved_two = normalize(second, norm_params, 1, cells)
    latent_mean = rows_times(two_low, latent_low[0]) + latent_bias[0]
    latent_logvar = rows_times(two_low, latent_low[1]) + latent_bias[1]
    spread_factor = jnp.exp(0.5 * latent_logvar)
    sample_low = low(latent_mean + all_noise * spread_factor)
    third = rows_times(sample_low, dec_in_low)
    three_low, saved_three = normalize(third, norm_params, 2, cells)
    fourth = rows_times(three_low, dec_mid_low)
    four_low, saved_four = normalize(fourth, norm_params, 3, cells)
    decoded = outer_cols(dec_out_turned, four_low) + bias_column
    error = decoded - counts_turned.astype(jnp.float32)
    gene_mask = rows_times(mask_turned, selection)
    loss_part = 0.5 / genes * jnp.sum(gene_mask * error * error)
    grad_decoded = low(gene_mask * error / genes)
    grad_four = inner_rows(grad_decoded, dec_out_turned)
    if whole:
        own_grad = own_rows(grad_decoded)
    else:
        loss_part, grad_four = lax.psum((loss_part, grad_four), "gene")
        own_grad = grad_decoded
    recon = low(rows_times(four_low, dec_out_low) + out_bias)
    kl_scale = ALPHA_KL / genes
    loss_part = loss_part + kl_scale * 0.5 * jnp.sum(
        jnp.exp(latent_logvar) + latent_mean * latent_mean - 1.0 - latent_logvar
    )
    grad_dec_out = rows_times(own_grad, four_low)
    grad_out_bias = jnp.sum(own_grad, axis=1, dtype=jnp.float32)

    def bias_rows(values):
        return lengthen(values.reshape(cell_count, -1), 1, hidden_width)

    pieces = [grad_dec_out, bias_rows(grad_out_bias)]
    moments = [mom_dec_out.T, bias_rows(mom_out_bias)]
    if whole:
        decoder = scatter_pieces(pieces, moments)
    else:
        own_moment_out, moment_bias = gather_slices(pieces, moments)
    grad_a4, gain_four, shift_four = norm_back(grad_four, saved_four, norm_params, 3, cells)
    together = lax.optimization_barrier
    half = jnp.bfloat16
    grad_three = outer_cols(grad_a4, dec_mid_low)
    if whole:
        grad_three, decoder = together((grad_three, decoder))
        decoder = gather_block(decoder)
    grad_a3, gain_three, shift_three = norm_back(grad_three, saved_three, norm_params, 2, cells)
    grad_sample = outer_cols(grad_a3, dec_in_low)
    grad_mean = low(grad_sample + kl_scale * latent_mean)
    grad_logvar = low(
        grad_sample * all_noise * 0.5 * spread_factor
        + kl_scale * 0.5 * (jnp.exp(latent_logvar) - 1.0)
    )
    grad_pair = jnp.concatenate([grad_mean, grad_logvar], axis=1)
    latent_pair = jnp.concatenate([latent_low[0], latent_low[1]], axis=1)
    grad_two = outer_cols(grad_pair, latent_pair)
    grad_dec_mid = inner_rows(three_low, grad_a4)
    grad_narrow = jnp.concatenate([inner_rows(grad_pair, two_low), inner_rows(sample_low, grad_a3)])
    grad_narrow = lengthen(grad_narrow, 0, 8 * cell_count)
    if whole:
        grad_two, grad_dec_mid, grad_narrow = together((grad_two, grad_dec_mid, grad_narrow))
        grad_dec_mid = halve(grad_dec_mid, 1, half)
        grad_narrow = halve(grad_narrow, 1, half)
    grad_a2, gain_two, shift_two = norm_back(grad_two, saved_two, norm_params, 1, cells)
    grad_one = outer_cols(grad_a2, enc_mid_low)
    if whole:
        grad_one, grad_narrow = together((grad_one, grad_narrow))
        grad_narrow = rounded(halve(grad_narrow, 2, half))
    grad_a1, gain_one, shift_one = norm_back(grad_one, saved_one, norm_params, 0, cells)
    grad_enc_in = inner_rows(counts, grad_a1)
    def finish_narrow(grad_narrow):
        grad_latent = grad_narrow[: 2 * latent_width].reshape(2, latent_width, hidden_width)
        grad_dec_in = grad_narrow[2 * latent_width : 3 * latent_width]
        new_mom_dec_in = MOMENTUM * mom_dec_in + grad_dec_in
        turned_latent = MOMENTUM * jnp.swapaxes(mom_latent_w, 1, 2) + grad_latent
        new_mom_latent_w = jnp.swapaxes(turned_latent, 1, 2)
        narrow = orthogonal_narrow(jnp.concatenate([turned_latent, new_mom_dec_in[None]]))
        return new_mom_dec_in, new_mom_latent_w, narrow

    grad_enc_in, grad_a2, grad_dec_mid, grad_narrow = together(
        (grad_enc_in, grad_a2, grad_dec_mid, grad_narrow)
    )
    if whole:
        encoder = rounded(scatter_pieces([grad_enc_in], [mom_enc_in], half))
    grad_enc_mid = inner_rows(one_low, grad_a2)
    small = jnp.concatenate([jnp.sum(grad_pair, axis=0, dtype=jnp.float32), loss_part[None]])
    if whole:
        grad_dec_mid = rounded(halve(grad_dec_mid, 2, half))
        grad_enc_mid = halve(grad_enc_mid, 1, half)
        grad_narrow = unite(grad_narrow, 2)
        encoder, decoder = together((encoder, decoder))
        moment_first = cut_pieces(gather_block(encoder), [gene_local])[0]
        grad_dec_mid, grad_enc_mid, grad_narrow = together(
            (grad_dec_mid, grad_enc_mid, grad_narrow)
        )
        grad_dec_mid = unite(grad_dec_mid, 2)
        grad_enc_mid = rounded(halve(grad_enc_mid, 2, half))
        grad_narrow = unite(grad_narrow, 1)
        grad_dec_mid, grad_enc_mid, grad_narrow = together(
            (grad_dec_mid, grad_enc_mid, grad_narrow)
        )
        grad_dec_mid = unite(grad_dec_mid, 1).astype(jnp.float32)
        grad_enc_mid = unite(grad_enc_mid, 2)
        finished = finish_narrow(grad_narrow.astype(jnp.float32))
        grad_dec_mid, grad_enc_mid, finished = together((grad_dec_mid, grad_enc_mid, finished))
        new_mom_dec_in, new_mom_latent_w, narrow = finished
        grad_enc_mid = unite(grad_enc_mid, 1)
        moment_out, moment_bias = cut_pieces(decoder, [gene_local, cell_count])
        own_moment_out = own_rows(moment_out)
    else:
        new_mom_enc_in = MOMENTUM * mom_enc_in + cell_sum(grad_enc_in)
        grad_enc_mid = cell_total(grad_enc_mid)
        grad_dec_mid = cell_total(grad_dec_mid)
        grad_narrow = cell_total(grad_narrow)
    if not whole:
        new_mom_dec_in, new_mom_latent_w, narrow = finish_narrow(grad_narrow)
    small = cell_sum(small)
    grad_latent_bias = small[: 2 * latent_width].reshape(2, latent_width)
    total = small[2 * latent_width]
    moment_bias = moment_bias[:, : gene_local // cell_count].reshape(gene_count, gene_local)
    new_mom_out_bias = lax.dynamic_index_in_dim(moment_bias, gene_at, 0, keepdims=False)
    new_out_bias = vector_step(out_bias, new_mom_out_bias, jnp.mean(moment_bias * moment_bias))
    new_mom_dec_out = own_moment_out.T

    if whole:
        grad_enc_mid = grad_enc_mid.astype(jnp.float32)
    new_mom_enc_mid = MOMENTUM * mom_enc_mid + grad_enc_mid
    new_mom_dec_mid = MOMENTUM * mom_dec_mid + grad_dec_mid
    factor = math.sqrt(max(1.0, hidden_width / latent_width))
    new_dec_in = dec_in - RATE * factor * narrow[2]
    new_latent_w = latent_w - RATE * jnp.swapaxes(narrow[:2], 1, 2)
    if whole:
        square = orthogonal_squares(new_mom_enc_mid, new_mom_dec_mid)
        done = (new_mom_enc_mid, new_mom_dec_mid, new_mom_latent_w, new_dec_in, new_latent_w)
        turned, moment_first, moment_out, done = together(
            (by_core(square), moment_first, moment_out, done)
        )
        new_mom_enc_mid, new_mom_dec_mid, new_mom_latent_w, new_dec_in, new_latent_w = done
        turned_enc_mid, turned_dec_mid = turned
        new_enc_mid = enc_mid - RATE * turned_enc_mid.astype(jnp.float32)
        new_dec_mid = dec_mid - RATE * turned_dec_mid.astype(jnp.float32)
        new_mom_enc_in = own_rows(moment_first).astype(jnp.float32)
        turned_in, turned_out = by_core(orthogonal_talls(moment_first, moment_out, gene_local))
    else:
        turned_in = orthogonal_shared(new_mom_enc_in)
        turned_out = orthogonal_shared(own_moment_out)
        new_enc_mid = enc_mid - RATE * orthogonal_shared(new_mom_enc_mid, ())
        new_dec_mid = dec_mid - RATE * orthogonal_shared(new_mom_dec_mid, ())
    new_enc_in = enc_in - RATE * turned_in.astype(jnp.float32)
    factor = math.sqrt(max(1.0, genes / hidden_width))
    new_dec_out = dec_out - RATE * factor * turned_out.astype(jnp.float32).T

    grad_norm = jnp.stack(
        [
            jnp.stack([gain_one, gain_two, gain_three, gain_four]),
            jnp.stack([shift_one, shift_two, shift_three, shift_four]),
        ]
    )
    new_mom_norm = MOMENTUM * mom_norm + grad_norm
    new_norm = vector_step(
        norm_params, new_mom_norm, jnp.mean(new_mom_norm * new_mom_norm, axis=-1, keepdims=True)
    )
    new_mom_latent_bias = MOMENTUM * mom_latent_bias + grad_latent_bias
    new_latent_bias = vector_step(
        latent_bias,
        new_mom_latent_bias,
        jnp.mean(new_mom_latent_bias * new_mom_latent_bias, axis=-1, keepdims=True),
    )
    means = jnp.stack([saved_one[2], saved_two[2], saved_three[2], saved_four[2]])
    variances = jnp.stack([saved_one[3], saved_two[3], saved_three[3], saved_four[3]])
    new_running_mean = 0.9 * running_mean + 0.1 * means
    updated_running_variance = 0.9 * running_variance + 0.1 * variances * (cells / (cells - 1.0))
    return (
        recon,
        total / cells,
        new_enc_in,
        new_mom_enc_in,
        new_enc_mid,
        new_mom_enc_mid,
        new_latent_w,
        new_mom_latent_w,
        new_dec_in,
        new_mom_dec_in,
        new_dec_mid,
        new_mom_dec_mid,
        new_dec_out,
        new_mom_dec_out,
        new_norm,
        new_mom_norm,
        new_latent_bias,
        new_mom_latent_bias,
        new_out_bias,
        new_mom_out_bias,
        new_running_mean,
        updated_running_variance,
    )


def solution(mesh):
    in_specs = (
        P("cell", "gene"),
        P("cell"),
        P(None, "gene"),
        P(("cell", "gene"), None),
        P("gene", None),
        P(),
        P(),
        P(),
        P(),
        P(None, "gene"),
        P(),
        P(),
        P("gene"),
        P(),
        P(),
        P("gene", None),
        P(),
        P(),
        P(),
        P(),
        P(None, "gene"),
        P(),
        P(),
        P("gene"),
    )
    out_specs = (
        P("cell", "gene"),
        P(),
        P("gene", None),
        P("gene", None),
        P(),
        P(),
        P(),
        P(),
        P(),
        P(),
        P(),
        P(),
        P(None, "gene"),
        P(None, "gene"),
        P(),
        P(),
        P(),
        P(),
        P("gene"),
        P("gene"),
        P(),
        P(),
    )
    return jax.shard_map(shards, mesh=mesh, in_specs=in_specs, out_specs=out_specs, check_vma=False)
```
